128 devices in a mesh: graph: 8 (over z, core), leaf: 16 (over y, x).
Axes of the slice: x: 4, y: 4, z: 4, core: 2. Of those that a mesh axis runs over, the one named last changes fastest.
Arguments:
- features: bfloat16 [1048576, 256], P(('graph', 'leaf')), may hold values from -6 to 6
- positions: float32 [3, 1048576], P(None, ('graph', 'leaf')), may hold values from -0.5 to 0.5
- energy_weight: float32 [1048576], P(('graph', 'leaf')), may hold values from -4 to 4
- send_slot: int32 [1048576], P(('graph', 'leaf')), may hold values from 0 to 8191, as said below
- tile_slot: int32 [1048576], P(('graph', 'leaf')), may hold values from 0 to 16383, as said below
- box_count: int32 [2048, 8], P('leaf', 'graph'), may hold values from 0 to 128, as said below
- list_box: int32 [2048, 64], P('leaf'), may hold values from 0 to 2047, as said below
- list_image: int32 [3, 2048, 64], P(None, 'leaf'), may hold values from -1 to 1
- w_in: bfloat16 [256, 256], replicated, may hold values from -0.375 to 0.375
- b_in: float32 [256], replicated, may hold values from -3 to 3
- w_mid: bfloat16 [256, 256], replicated, may hold values from -0.375 to 0.375
- b_mid: float32 [256], replicated, may hold values from -3 to 3
- w_out: bfloat16 [256], replicated, may hold values from -0.375 to 0.375
Outputs:
- feature_grad: bfloat16 [1048576, 256], P(('graph', 'leaf'))
- position_grad: float32 [3, 1048576], P(None, ('graph', 'leaf'))
- in_grad: float32 [256, 256], replicated
- in_bias_grad: float32 [256], replicated
- mid_grad: float32 [256, 256], replicated
- mid_bias_grad: float32 [256], replicated
- out_grad: float32 [256], replicated
The draws below stay inside these ranges and needn't reach their ends.
Inputs may be any that keep to these rules, and one draw needn't show every extreme that they name: On each device send_slot is a permutation of 0 to 8191, so each device sends 64 atoms to every device. On each device the tile_slot values are distinct and are exactly the live slots b * 128 + k, k < box_count of that device's box b. `box_count`: the counts of one device sum to 8192. list_box[b, k] is the box at grid offset d_bk from box b, wrapped periodically, where d_bk has largest component magnitude exactly 2 and the 64 offsets of a box are distinct; list_image is the number of wraps along each dimension.
All inputs are finite; a program needn't handle non-finite values.
Results may differ from the reference program's by a relative error of at most 0.015.
Values may be sent and summed in bfloat16 or wider, within the bound.
A program may use at most 192 MiB of HBM per device.

```python
import jax
import jax.numpy as jnp
import numpy as np
from jax import lax

FEAT = 256
HID = 256
LIST = 64
BOX_DEV = 128
SLOT_DEV = 128
ATOM_DEV = 8192
CAP = 64
ATOMS = 1048576
NBOX = 2048
N_GRAPH = 8
N_LEAF = 16
DEVICES = 128


def shell_table():
    spans = np.arange(-2, 3)
    cube = np.stack(np.meshgrid(spans, spans, spans, indexing='ij'), -1).reshape(-1, 3)
    return cube[np.abs(cube).max(1) == 2]


def tile_layout(key):
    key = jax.random.fold_in(key, 7)
    subkeys = jax.random.split(key, 3)
    half_boxes = BOX_DEV // 2
    first_half = jax.random.randint(subkeys[0], (DEVICES, half_boxes), 0, SLOT_DEV + 1)
    first_half = first_half.at[:, 0].set(SLOT_DEV)
    counts = jnp.concatenate([first_half, SLOT_DEV - first_half], 1)
    shuffle = jax.vmap(lambda subkey: jax.random.permutation(subkey, BOX_DEV))(jax.random.split(subkeys[1], DEVICES))
    counts = jnp.take_along_axis(counts, shuffle, 1)
    all_slots = jnp.arange(BOX_DEV * SLOT_DEV)
    live_mask = all_slots[None] % SLOT_DEV < jnp.repeat(counts, SLOT_DEV, 1)
    scores = jnp.where(live_mask, all_slots[None], all_slots[None] + BOX_DEV * SLOT_DEV)
    ranked = jnp.argsort(scores, axis=1)[:, :ATOM_DEV]
    mixing = jax.vmap(lambda subkey: jax.random.permutation(subkey, ATOM_DEV))(jax.random.split(subkeys[2], DEVICES))
    tile_order = jnp.take_along_axis(ranked, mixing, 1)
    return (counts, tile_order)


def list_layout(key):
    key = jax.random.fold_in(key, 9)
    shell = jnp.asarray(shell_table(), jnp.int32)
    chosen = jax.vmap(lambda subkey: jax.random.permutation(subkey, shell.shape[0])[:LIST])(jax.random.split(key, NBOX))
    offsets = shell[chosen]
    box_ids = jnp.arange(NBOX, dtype=jnp.int32)
    coords = jnp.stack([box_ids % 8, box_ids // 8 % 8, box_ids // 64], -1)
    grid_dims = jnp.array([8, 8, NBOX // 64], jnp.int32)
    shifted = coords[:, None, :] + offsets
    wraps = jnp.floor_divide(shifted, grid_dims)
    wrapped = shifted - wraps * grid_dims
    flat_index = wrapped[..., 0] + 8 * wrapped[..., 1] + 64 * wrapped[..., 2]
    return (flat_index.astype(jnp.int32), jnp.transpose(wraps, (2, 0, 1)).astype(jnp.int32))


def draw_send_slot(key, part):
    key = jax.random.fold_in(key, 5)
    orders = jax.vmap(lambda subkey: jax.random.permutation(subkey, ATOM_DEV))(jax.random.split(key, DEVICES))
    return orders.reshape(ATOMS).astype(jnp.int32)


def draw_tile_slot(key, part):
    counts, tile_order = tile_layout(key)
    return tile_order.reshape(ATOMS).astype(jnp.int32)


def draw_box_count(key, part):
    counts, tile_order = tile_layout(key)
    return counts.reshape(N_GRAPH, N_LEAF, BOX_DEV).transpose(1, 2, 0).reshape(NBOX, N_GRAPH).astype(jnp.int32)


def draw_list_box(key, part):
    flat_index, wraps = list_layout(key)
    return flat_index


def draw_list_image(key, part):
    flat_index, wraps = list_layout(key)
    return wraps


def level_of(key, shape, cuts, smallest, largest):
    factor_of = 1.0
    for position, parts in cuts:
        heights = jax.random.uniform(jax.random.fold_in(jax.random.fold_in(key, 6), position), (parts,), jnp.float32, smallest / len(cuts), largest / len(cuts))
        factor_of = factor_of * jnp.repeat(jnp.exp(heights), shape[position] // parts).reshape((-1,) + (1,) * (len(shape) - 1 - position))
    return factor_of


def normal_values(key, shape, width, bound, cuts=(), kind=jnp.bfloat16):
    entries = jax.random.normal(key, shape, jnp.float32) * width
    if len(cuts) > 0:
        entries = level_of(key, shape, cuts, -0.22, 0.18) * entries
    return jnp.clip(entries, min=-bound, max=bound).astype(kind)


def setup_inputs(seed: int = 0) -> dict:
    streams_of = jax.random.split(jax.random.key(seed), 14)
    features = normal_values(streams_of[0], (ATOMS, FEAT), 1.0, 6.0, ((0, 128),))
    positions = jnp.clip(jax.random.uniform(streams_of[1], (3, ATOMS), jnp.float32, -0.5, 0.5) * level_of(streams_of[1], (3, ATOMS), ((1, 128),), -0.4, 0.0), -0.5, 0.5)
    energy_weight = normal_values(streams_of[2], (ATOMS,), 1.0, 4.0, ((0, 128),), jnp.float32)
    send_slot = draw_send_slot(jax.random.fold_in(streams_of[13], 71), 0)
    tile_slot = draw_tile_slot(jax.random.fold_in(streams_of[13], 71), 0)
    box_count = draw_box_count(jax.random.fold_in(streams_of[13], 71), 0)
    list_box = draw_list_box(jax.random.fold_in(streams_of[13], 71), 0)
    list_image = draw_list_image(jax.random.fold_in(streams_of[13], 71), 0)
    w_in = normal_values(streams_of[8], (FEAT, HID), FEAT ** -0.5, 0.375)
    b_in = normal_values(streams_of[9], (HID,), 0.5, 3.0, (), jnp.float32)
    w_mid = normal_values(streams_of[10], (HID, HID), HID ** -0.5, 0.375)
    b_mid = normal_values(streams_of[11], (HID,), 0.5, 3.0, (), jnp.float32)
    w_out = normal_values(streams_of[12], (HID,), HID ** -0.5, 0.375)
    return {"features": features, "positions": positions, "energy_weight": energy_weight, "send_slot": send_slot, "tile_slot": tile_slot, "box_count": box_count, "list_box": list_box, "list_image": list_image, "w_in": w_in, "b_in": b_in, "w_mid": w_mid, "b_mid": b_mid, "w_out": w_out}


coupling = 0.5

def silu_slope(pre_act):
    sigmoid_z = jax.nn.sigmoid(pre_act)
    return sigmoid_z * (1.0 + pre_act * (1.0 - sigmoid_z))

def box_coords(box_ids):
    return jnp.stack([box_ids % 8, box_ids // 8 % 8, box_ids // 64], 0).astype(jnp.float32)

def kernel_parts(separation):
    dist_sq = lax.optimization_barrier(jnp.sum(separation * separation, 0))
    inverse = lax.rsqrt(dist_sq)
    return (inverse, inverse * inverse * inverse, dist_sq)

def translate(separation, sources):
    inverse, inverse_cube, dist_sq = kernel_parts(separation)
    projected = lax.optimization_barrier(jnp.sum(separation * sources[1:], 0))
    potential_part = sources[0] * inverse - projected * inverse_cube
    gradient = sources[0] * separation * inverse_cube + (sources[1:] - 3.0 * separation * projected / dist_sq) * inverse_cube
    return jnp.concatenate([potential_part[None], gradient], 0)

def translate_back(separation, targets):
    inverse, inverse_cube, dist_sq = kernel_parts(separation)
    target_zero = targets[0][:, None]
    target_grad = targets[1:][:, :, None]
    projected = lax.optimization_barrier(jnp.sum(separation * target_grad, 0))
    potential_part = target_zero * inverse + projected * inverse_cube
    gradient = -target_zero * separation * inverse_cube + (target_grad - 3.0 * separation * projected / dist_sq) * inverse_cube
    return jnp.concatenate([potential_part[None], gradient], 0)

def head_forward(row_block, w_in, b_in, w_mid, b_mid, w_out):
    pre_one = jnp.dot(row_block, w_in, preferred_element_type=jnp.float32) + b_in
    act_one = jax.nn.silu(pre_one).astype(jnp.bfloat16)
    pre_two = jnp.dot(act_one, w_mid, preferred_element_type=jnp.float32) + b_mid
    act_two = jax.nn.silu(pre_two).astype(jnp.bfloat16)
    charge = jnp.dot(act_two, w_out, preferred_element_type=jnp.float32)
    return (pre_one, act_one, pre_two, act_two, charge)

def head_backward(row_block, pre_one, act_one, pre_two, act_two, grad_bf, w_in, w_mid, w_out):
    contract_rows = (((0,), (0,)), ((), ()))
    contract_cols = (((1,), (1,)), ((), ()))
    out_grad = jnp.dot(grad_bf, act_two, preferred_element_type=jnp.float32)
    mid_slope = (grad_bf.astype(jnp.float32)[:, None] * w_out.astype(jnp.float32)[None] * silu_slope(pre_two)).astype(jnp.bfloat16)
    mid_grad = lax.dot_general(act_one, mid_slope, contract_rows, preferred_element_type=jnp.float32)
    mid_bias = lax.optimization_barrier(jnp.sum(mid_slope, 0, dtype=jnp.float32))
    back_one = lax.dot_general(mid_slope, w_mid, contract_cols, preferred_element_type=jnp.float32)
    in_slope = (back_one * silu_slope(pre_one)).astype(jnp.bfloat16)
    in_grad = lax.dot_general(row_block, in_slope, contract_rows, preferred_element_type=jnp.float32)
    in_bias = lax.optimization_barrier(jnp.sum(in_slope, 0, dtype=jnp.float32))
    row_grad = lax.dot_general(in_slope, w_in, contract_cols, preferred_element_type=jnp.float32).astype(jnp.bfloat16)
    return (row_grad, (in_grad, in_bias, mid_grad, mid_bias, out_grad))

def reference(features, positions, energy_weight, send_slot, tile_slot, box_count, list_box, list_image, w_in, b_in, w_mid, b_mid, w_out):
    atom_ids = jnp.arange(ATOMS, dtype=jnp.int32)
    dest_dev = (send_slot // CAP).astype(jnp.int32)
    recv_row = (atom_ids // ATOM_DEV * CAP + send_slot % CAP).astype(jnp.int32)
    tile_pos = tile_slot[dest_dev * ATOM_DEV + recv_row]
    atom_box = (dest_dev % N_LEAF * BOX_DEV + tile_pos // SLOT_DEV).astype(jnp.int32)
    graph_idx = (dest_dev // N_LEAF).astype(jnp.int32)
    live_mask = (tile_pos % SLOT_DEV < box_count[atom_box, graph_idx]).astype(jnp.float32)
    blocks = features.reshape(DEVICES, ATOM_DEV, FEAT)
    charge = lax.map(lambda block: head_forward(block, w_in, b_in, w_mid, b_mid, w_out)[4], blocks).reshape(ATOMS) * live_mask
    weighted = 0.5 * coupling * energy_weight * charge
    ones_pos = jnp.concatenate([jnp.ones((1, ATOMS), jnp.float32), positions], 0)
    moments = jax.ops.segment_sum((charge * ones_pos).T, atom_box, NBOX).T
    local_bar = jax.ops.segment_sum((weighted * ones_pos).T, atom_box, NBOX).T
    own_boxes = jnp.arange(NBOX, dtype=jnp.int32)
    grid_dims = jnp.array([8.0, 8.0, NBOX // 64], jnp.float32).reshape(3, 1, 1)
    separation = box_coords(list_box) + list_image.astype(jnp.float32) * grid_dims - box_coords(own_boxes)[:, :, None]
    local_exp = lax.optimization_barrier(jnp.sum(translate(separation, moments[:, list_box]), -1))
    back_terms = translate_back(separation, local_bar)
    moment_bar = jax.ops.segment_sum(back_terms.reshape(4, -1).T, list_box.reshape(-1), NBOX).T
    at_box = local_exp[:, atom_box]
    bar_box = moment_bar[:, atom_box]
    potential = at_box[0] + lax.optimization_barrier(jnp.sum(at_box[1:] * positions, 0))
    grad_q = (0.5 * coupling * energy_weight * potential + bar_box[0] + lax.optimization_barrier(jnp.sum(bar_box[1:] * positions, 0))) * live_mask
    position_grad = weighted * at_box[1:] + charge * bar_box[1:]
    grad_bf = grad_q.astype(jnp.bfloat16).reshape(DEVICES, ATOM_DEV)

    def accumulate(totals, pieces):
        block, grad_block = pieces
        pre_one, act_one, pre_two, act_two, unused = head_forward(block, w_in, b_in, w_mid, b_mid, w_out)
        row_grad, weight_grads = head_backward(block, pre_one, act_one, pre_two, act_two, grad_block, w_in, w_mid, w_out)
        return (tuple((left + right for left, right in zip(totals, weight_grads))), row_grad)
    initial = (jnp.zeros((FEAT, HID), jnp.float32), jnp.zeros((HID,), jnp.float32), jnp.zeros((HID, HID), jnp.float32), jnp.zeros((HID,), jnp.float32), jnp.zeros((HID,), jnp.float32))
    totals, row_grads = lax.scan(accumulate, initial, (blocks, grad_bf))
    return (row_grads.reshape(ATOMS, FEAT), position_grad, totals[0], totals[1], totals[2], totals[3], totals[4])
```

```python
import functools

import jax
import jax.numpy as jnp
from jax import lax
from jax.experimental import pallas as pl
from jax.experimental.pallas import tpu as pltpu
from jax.sharding import PartitionSpec as P

MESH = pl.DeviceIdType.MESH
F32 = jnp.float32
BF16 = jnp.bfloat16
COUPLING = 0.5
SLOT_DEV = 128
NT = (((1,), (1,)), ((), ()))
NN = (((1,), (0,)), ((), ()))
TN = (((0,), (0,)), ((), ()))


def mm(a, b, dims=NN):
    return lax.dot_general(a, b, dims, preferred_element_type=F32)


def iota(shape, axis):
    return lax.broadcasted_iota(jnp.int32, shape, axis)


def tile_lanes(x, n):
    return jnp.concatenate([x] * (n // x.shape[1]), 1)


def fold_lanes(x):
    parts = [x[:, i : i + 128] for i in range(0, x.shape[1], 128)]
    total = parts[0]
    for part in parts[1:]:
        total = total + part
    return total


def roll(x, shift):
    return pltpu.roll(x, shift % 128, 1)


def shift_x(x):
    first = roll(pltpu.roll(x, 120, 1, stride=1, stride_axis=0), 6)
    col = iota(x.shape, 1) % 8 + 2 - iota(x.shape, 0)
    return jnp.where(col > 7, roll(first, 8), jnp.where(col < 0, roll(first, -8), first))


def shift_y(x, dy):
    if dy == 0:
        return x
    straight = roll(x, -8 * dy)
    row = (iota(x.shape, 1) // 8) % 8 + dy
    return jnp.where((row >= 0) & (row < 8), straight, roll(straight, 64))


def shift_z(slabs, dz):
    if dz % 2 == 0:
        return slabs[dz // 2 + 1]
    low, high = (0, 1) if dz == -1 else (1, 2)
    lower = iota(slabs[0].shape, 1) < 64
    return jnp.where(lower, roll(slabs[low], 64), roll(slabs[high], 64))


def kernel(
    n_graph, n_leaf, chunk, n_grp,
    feat, pos, ew, sslot, tslot, count, lbox, limg, w_in, b_in, w_mid, b_mid, w_out,
    fgrad, pgrad, ing, inb, midg, midb, outg,
    X, A1, SL1, A2, SL2, OB, U, Q, W1H, W1T, W2TH, W2H, B1, B2, WO, WOH,
    CODE, CA, CB, CS, F, G, GN, R, LCODE, MX, P1, S1, P2, TO, TB,
    MIDACC, INACC, OGACC, IBACC, MIDS, INS, RM, RI, GS, GM, AS, AM, BV, BL, BS, BG,
    xsem, osem, ssem, rsem,
):
    g = lax.axis_index("graph")
    l = lax.axis_index("leaf")
    atoms = X.shape[0]
    hid = SL1.shape[0]
    cap = atoms // (n_graph * n_leaf)
    leaf_bits = n_leaf.bit_length() - 1
    cap_bits = cap.bit_length() - 1
    code_rows = n_leaf * cap // 128
    box_dev = 128
    wrow = hid // n_leaf

    def leaf_peer(o):
        return lax.rem(l + o, n_leaf)

    def graph_peer(o):
        return lax.rem(g + o, n_graph)

    def to_leaf(k, src_of, dst):
        @pl.loop(1, n_leaf)
        def _(o):
            peer = leaf_peer(o)
            pltpu.make_async_remote_copy(
                src_ref=src_of(peer), dst_ref=dst, send_sem=ssem.at[k], recv_sem=rsem.at[k],
                device_id=(g, peer), device_id_type=MESH,
            ).start()

    def to_graph(k, src_of, dst):
        @pl.loop(1, n_graph)
        def _(o):
            peer = graph_peer(o)
            pltpu.make_async_remote_copy(
                src_ref=src_of(peer), dst_ref=dst, send_sem=ssem.at[k], recv_sem=rsem.at[k],
                device_id=(peer, l), device_id_type=MESH,
            ).start()

    def wait_on(sem, view):
        pltpu.make_async_copy(view, view, sem).wait()

    bar = pltpu.get_barrier_semaphore()

    @pl.loop(1, n_leaf)
    def _(o):
        pl.semaphore_signal(bar, inc=1, device_id=(g, leaf_peer(o)), device_id_type=MESH)

    @pl.loop(1, n_graph)
    def _(o):
        pl.semaphore_signal(bar, inc=1, device_id=(graph_peer(o), l), device_id_type=MESH)

    n_chunks = atoms // chunk

    def feat_copy(c):
        rows = pl.ds(c * chunk, chunk)
        return pltpu.make_async_copy(feat.at[rows], X.at[rows], xsem.at[c])

    @pl.loop(0, n_chunks)
    def _(c):
        feat_copy(c).start()

    slot = tslot[...]
    box = slot >> 7

    def count_step(b, cnt):
        return jnp.where(box == b, count[b, 0], cnt)

    cnt = lax.fori_loop(0, box_dev, count_step, jnp.zeros_like(slot), unroll=8)
    CODE[...] = jnp.where((slot & (SLOT_DEV - 1)) < cnt, box, -1).astype(F32)

    pl.semaphore_wait(bar, n_leaf + n_graph - 2)
    CA[g] = CODE[pl.ds(pl.multiple_of(g * code_rows, code_rows), code_rows), :]
    to_graph(
        0,
        lambda peer: CODE.at[pl.ds(pl.multiple_of(peer * code_rows, code_rows), code_rows)],
        CA.at[g],
    )

    own = l * box_dev + iota((box_dev, lbox.shape[1]), 0)
    src = lbox[...]
    dims = (8, 8, n_leaf * box_dev // 64)
    dx, dy, dz = [
        coord(src) + limg[i] * dims[i] - coord(own)
        for i, coord in enumerate([lambda b: b & 7, lambda b: (b >> 3) & 7, lambda b: b >> 6])
    ]
    code = (((dz + 2) * 5 + dy + 2) * 8 + 2 - dx).astype(F32)
    code = jnp.concatenate([code, jnp.zeros((box_dev, 128 - code.shape[1]), F32)], 1)
    LCODE[...] = code.T.astype(jnp.int32)
    F[...] = jnp.zeros_like(F)
    sub = iota((8, 128), 0)

    def mask_step(k, masks):
        row = LCODE[pl.ds(k, 1), :] - sub
        return tuple(m + jnp.where(row == 8 * i, 1.0, 0.0) for i, m in enumerate(masks))

    masks = lax.fori_loop(
        0, lbox.shape[1], mask_step, tuple(jnp.zeros((8, 128), F32) for _ in range(n_grp)), unroll=4
    )
    G[...] = jnp.zeros_like(G)
    for i in range(n_grp):
        F[8 * i : 8 * i + 8, :] = masks[i]
    for i in range(n_grp):
        for j in range(5):
            other = 8 * (n_grp - 1 - i) + 4 - j
            G[8 * i + j : 8 * i + j + 1, :] = F[other : other + 1, :]
    for k, step in ((2, 1), (3, n_leaf - 1)):
        pltpu.make_async_remote_copy(
            src_ref=G, dst_ref=GN.at[k - 2], send_sem=ssem.at[k], recv_sem=rsem.at[k],
            device_id=(g, leaf_peer(step)), device_id_type=MESH,
        ).start()

    w1 = w_in[...].astype(F32).T
    W1T[...] = w1.astype(BF16)
    W1H[...] = (0.5 * w1).astype(BF16)
    w2 = w_mid[...].astype(F32)
    W2H[...] = (0.5 * w2).astype(BF16)
    W2TH[...] = (0.5 * w2.T).astype(BF16)

    def column(row):
        return jnp.broadcast_to(row, (128, hid)).T

    B1[...] = column(0.5 * b_in[...])
    B2[...] = column(0.5 * b_mid[...])
    wo = column(w_out[...].astype(F32))
    WO[...] = wo
    WOH[...] = 0.5 * wo
    A1[hid:, :] = jnp.ones((A1.shape[0] - hid, atoms), BF16)
    U[...] = jnp.ones_like(U)
    U[1:4, :] = pos[...]
    U[5:8, :] = pos[...]

    def head(c):
        feat_copy(c).wait()
        cols = pl.ds(pl.multiple_of(c * chunk, chunk), chunk)
        h = mm(W1H[...], X[pl.ds(pl.multiple_of(c * chunk, chunk), chunk), :], NT)
        h = h + tile_lanes(B1[...], chunk)
        t = jnp.tanh(h)
        p = h * t
        a = (h + p).astype(BF16)
        A1[:hid, cols] = a
        SL1[:, cols] = ((1.0 + t) * (1.0 + (h - p))).astype(BF16)
        h = mm(W2TH[...], a) + tile_lanes(B2[...], chunk)
        t = jnp.tanh(h)
        p = h * t
        a = h + p
        A2[:, cols] = a.astype(BF16)
        SL2[:, cols] = (
            tile_lanes(WOH[...], chunk) * ((1.0 + t) * (1.0 + (h - p)))
        ).astype(BF16)
        Q[:, cols] = jnp.sum(a * tile_lanes(WO[...], chunk), 0, keepdims=True)

    first = n_chunks // 2
    pl.loop(0, first)(head)

    wait_on(rsem.at[0], CA.at[pl.ds(0, n_graph - 1)])
    flat = CA[...]
    for r in range(code_rows):
        CB[r] = flat[:, r, :]
    half = 128 // cap
    CS[l] = CB[l // half]
    to_leaf(1, lambda peer: CB.at[peer // half], CS.at[l])

    wait_on(rsem.at[2], GN.at[0])
    wait_on(rsem.at[3], GN.at[1])
    for i in range(n_grp):
        at = pl.ds(8 * i, 8)
        slabs = [shift_x(x) for x in (GN[0, at, :], G[at, :], GN[1, at, :])]
        R[at, :] = shift_y(shift_z(slabs, i // 5 - 2), i % 5 - 2)

    pl.loop(first, n_chunks)(head)

    wait_on(rsem.at[1], CS.at[pl.ds(0, n_leaf - 1)])
    codes = CS[...].reshape(n_leaf * n_graph, 128).T
    mine = codes[:cap]
    for i in range(1, half):
        mine = jnp.where(lax.rem(l, half) == i, codes[i * cap : (i + 1) * cap], mine)
    mine = mine.astype(BF16)
    MIDACC[...] = jnp.zeros_like(MIDACC)
    macc = MIDACC.at[pl.ds(0, 2 * n_leaf * 8), pl.ds(0, 128)]

    def scale_row(cols):
        return (0.5 * COUPLING) * ew[:, cols]

    def one_hot(index, n):
        return jnp.where(iota((n, chunk), 0) == index, 1.0, 0.0).astype(BF16)

    def place(c):
        cols = pl.ds(pl.multiple_of(c * chunk, chunk), chunk)
        s = sslot[:, cols]
        src_leaf = (s >> cap_bits) & (n_leaf - 1)
        row = src_leaf * n_graph + (s >> (cap_bits + leaf_bits))
        picked = mm(mine, one_hot(row, n_leaf * n_graph))
        in_row = iota((cap, chunk), 0) == (s & (cap - 1))
        atom_box = jnp.sum(jnp.where(in_row, picked, 0.0), 0, keepdims=True)
        ob = one_hot(atom_box.astype(jnp.int32), box_dev)
        OB[:, cols] = ob
        q = Q[:, cols]
        sub = iota((8, chunk), 0)
        vals = U[:, cols] * jnp.where(sub < 4, q, scale_row(cols) * q)
        hi = vals.astype(BF16).astype(F32)
        lo = vals - hi
        blocks = [jnp.where(src_leaf == i, hi, 0.0) for i in range(n_leaf)]
        blocks += [jnp.where(src_leaf == i, lo, 0.0) for i in range(n_leaf)]
        macc[...] += mm(jnp.concatenate(blocks, 0).astype(BF16), ob, NT)

    pl.loop(0, n_chunks)(place)

    rows = n_leaf * 8
    part = macc[:rows, :] + macc[rows:, :]
    MX[8 : rows + 8, :] = part
    MX[:8, :] = part[rows - 8 :]
    MX[rows + 8 :, :] = part[:8]
    P1[l] = MX[pl.ds(pl.multiple_of(l * 8, 8), 24), :]
    to_leaf(4, lambda peer: MX.at[pl.ds(pl.multiple_of(peer * 8, 8), 24)], P1.at[l])
    wait_on(rsem.at[4], P1.at[pl.ds(0, n_leaf - 1)])
    total = jnp.sum(P1[...], 0)
    S1[...] = total
    P2[g] = total
    to_graph(5, lambda peer: S1, P2.at[g])
    wait_on(rsem.at[5], P2.at[pl.ds(0, n_graph - 1)])
    total = jnp.sum(P2[...], 0)

    shifted = []
    for ch in range(8):
        slabs = [
            shift_x(jnp.broadcast_to(total[8 * s + ch : 8 * s + ch + 1], (8, 128))) for s in range(3)
        ]
        shifted.append([shift_z(slabs, d) for d in range(-2, 3)])
    off_x = (2 - iota((8, 128), 0)).astype(F32)
    sums = [jnp.zeros((8, 128), F32) for _ in range(8)]
    for i in range(n_grp):
        off_z, off_y = i // 5 - 2, i % 5 - 2
        dist = jnp.maximum(off_x * off_x + float(off_z * off_z + off_y * off_y), 1.0)
        inv = lax.rsqrt(dist)
        cube = inv * inv * inv
        three = 3.0 * inv * inv
        for base, mask in ((0, F), (4, R)):
            m = mask[8 * i : 8 * i + 8, :]
            q0, q1, q2, q3 = [
                m * shift_y(shifted[base + j][off_z + 2], off_y) for j in range(4)
            ]
            proj = off_x * q1 + float(off_y) * q2 + float(off_z) * q3
            sums[base] += q0 * inv - proj * cube
            radial = q0 - three * proj
            sums[base + 1] += (radial * off_x + q1) * cube
            sums[base + 2] += (radial * float(off_y) + q2) * cube
            sums[base + 3] += (radial * float(off_z) + q3) * cube
    for j in range(8):
        TO[j : j + 1, :] = jnp.sum(sums[j], 0, keepdims=True)
    TB[l] = TO[...]
    to_leaf(6, lambda peer: TO, TB.at[l])
    wait_on(rsem.at[6], TB.at[pl.ds(0, n_leaf - 1)])
    table = TB[...].reshape(rows, 128)
    hi = table.astype(BF16)
    table = jnp.concatenate([hi, (table - hi.astype(F32)).astype(BF16)], 0)

    MIDACC[...] = jnp.zeros_like(MIDACC)
    INACC[...] = jnp.zeros_like(INACC)
    OGACC[...] = jnp.zeros_like(OGACC)
    IBACC[...] = jnp.zeros_like(IBACC)

    def backward_mid(c):
        cols = pl.ds(pl.multiple_of(c * chunk, chunk), chunk)
        src_leaf = (sslot[:, cols] >> cap_bits) & (n_leaf - 1)
        got = mm(table, OB[:, cols])
        got = got[:rows] + got[rows:]
        field = jnp.zeros((8, chunk), F32)
        for i in range(n_leaf):
            field += jnp.where(src_leaf == i, got[8 * i : 8 * i + 8], 0.0)
        sub = iota((8, chunk), 0)
        terms = field * U[:, cols]
        q = Q[:, cols]
        w = scale_row(cols)
        grad = jnp.sum(terms * jnp.where(sub < 4, w, 1.0), 0, keepdims=True)
        force = field * jnp.where(sub < 4, w * q, q)
        force = force + pltpu.roll(force, 4, 0)
        pgrad[:, cols] = force[1:4]
        grad = jnp.broadcast_to(grad, (16, chunk)).astype(BF16)
        ms = SL2[:, cols].reshape(hid // 16, 16, chunk) * grad[None]
        ms = ms.reshape(hid, chunk)
        SL2[:, cols] = ms
        MIDACC[...] += mm(A1[:, cols], ms, NT)
        og = A2[:, cols].reshape(hid // 16, 16, chunk) * grad[None]
        OGACC[...] += fold_lanes(og.reshape(hid, chunk).astype(F32))

    pl.loop(0, n_chunks)(backward_mid)

    def shares(src, sems, dst):
        dst[l] = src[pl.ds(pl.multiple_of(l * wrow, wrow), wrow), :]
        to_leaf(sems, lambda peer: src.at[pl.ds(pl.multiple_of(peer * wrow, wrow), wrow)], dst.at[l])

    MIDS[...] = MIDACC[:hid, :].astype(BF16)
    shares(MIDS, 7, RM)

    def backward_in(c):
        cols = pl.ds(pl.multiple_of(c * chunk, chunk), chunk)
        slope = mm(W2H[...], SL2[:, cols]) * SL1[:, cols].astype(F32)
        IBACC[...] += fold_lanes(slope)
        slope = slope.astype(BF16)
        SL1[:, cols] = slope
        INACC[...] += mm(slope, X[pl.ds(pl.multiple_of(c * chunk, chunk), chunk), :])

    pl.loop(0, n_chunks)(backward_in)
    INS[...] = INACC[...].astype(BF16)
    shares(INS, 8, RI)

    def to_row(columns):
        return jnp.sum(columns.T, 0, keepdims=True)

    BV[...] = jnp.zeros_like(BV)
    vectors = (MIDACC[hid : hid + 1, :], to_row(OGACC[...]), to_row(IBACC[...]))
    for i, vector in enumerate(vectors):
        for j in range(hid // 128):
            at = 2 * i + j
            BV[at : at + 1, :] = vector[:, 128 * j : 128 * j + 128]
    BL[l] = BV[...]
    to_leaf(9, lambda peer: BV, BL.at[l])

    def out_copy(c):
        rows = pl.ds(c * chunk, chunk)
        return pltpu.make_async_copy(X.at[rows], fgrad.at[rows], osem.at[c])

    def backward_row(c):
        at = pl.ds(pl.multiple_of(c * chunk, chunk), chunk)
        X[at, :] = mm(SL1[:, at], W1T[...], TN).astype(BF16)
        out_copy(c).start()

    cut = [n_chunks * i // 4 for i in range(5)]
    pl.loop(cut[0], cut[1])(backward_row)

    wait_on(rsem.at[7], RM.at[pl.ds(0, n_leaf - 1)])
    wait_on(rsem.at[8], RI.at[pl.ds(0, n_leaf - 1)])
    wait_on(rsem.at[9], BL.at[pl.ds(0, n_leaf - 1)])
    GS[:wrow, :] = jnp.sum(RM[...].astype(F32), 0).astype(BF16)
    GS[wrow:, :] = jnp.sum(RI[...].astype(F32), 0).astype(BF16)
    GM[g] = GS[...]
    BS[...] = jnp.sum(BL[...], 0)
    BG[g] = BS[...]
    to_graph(10, lambda peer: GS, GM.at[g])
    to_graph(11, lambda peer: BS, BG.at[g])
    pl.loop(cut[1], cut[2])(backward_row)
    wait_on(rsem.at[10], GM.at[pl.ds(0, n_graph - 1)])
    wait_on(rsem.at[11], BG.at[pl.ds(0, n_graph - 1)])
    AS[...] = jnp.sum(GM[...].astype(F32), 0).astype(BF16)
    AM[l] = AS[...]
    to_leaf(12, lambda peer: AS, AM.at[l])
    bias = jnp.sum(BG[...], 0)
    for i, out in enumerate((midb, outg, inb)):
        for j in range(hid // 128):
            out[:, 128 * j : 128 * j + 128] = bias[2 * i + j : 2 * i + j + 1]
    pl.loop(cut[2], cut[4])(backward_row)
    wait_on(rsem.at[12], AM.at[pl.ds(0, n_leaf - 1)])
    midg[...] = AM[:, :wrow, :].astype(F32).reshape(hid, hid)
    ing[...] = AM[:, wrow:, :].astype(F32).reshape(hid, hid).T

    wait_on(ssem.at[0], CA.at[pl.ds(0, n_graph - 1)])
    wait_on(ssem.at[1], CS.at[pl.ds(0, n_leaf - 1)])
    wait_on(ssem.at[2], GN.at[0])
    wait_on(ssem.at[3], GN.at[1])
    wait_on(ssem.at[4], P1.at[pl.ds(0, n_leaf - 1)])
    wait_on(ssem.at[5], P2.at[pl.ds(0, n_graph - 1)])
    wait_on(ssem.at[6], TB.at[pl.ds(0, n_leaf - 1)])
    wait_on(ssem.at[7], RM.at[pl.ds(0, n_leaf - 1)])
    wait_on(ssem.at[8], RI.at[pl.ds(0, n_leaf - 1)])
    wait_on(ssem.at[9], BL.at[pl.ds(0, n_leaf - 1)])
    wait_on(ssem.at[10], GM.at[pl.ds(0, n_graph - 1)])
    wait_on(ssem.at[11], BG.at[pl.ds(0, n_graph - 1)])
    wait_on(ssem.at[12], AM.at[pl.ds(0, n_leaf - 1)])

    @pl.loop(0, n_chunks)
    def _(c):
        out_copy(c).wait()


def body(
    features, positions, energy_weight, send_slot, tile_slot, box_count, list_box, list_image,
    w_in, b_in, w_mid, b_mid, w_out,
):
    n_graph, n_leaf = lax.axis_size("graph"), lax.axis_size("leaf")
    atoms, feat = features.shape
    hid = w_in.shape[1]
    chunk = min(512, atoms // 4)
    n_grp = 25
    code_rows = n_leaf * (atoms // (n_graph * n_leaf)) // 128
    wrow = hid // n_leaf
    vmem = pl.BlockSpec(memory_space=pltpu.VMEM)
    any_space = pl.BlockSpec(memory_space=pl.ANY)
    smem = pl.BlockSpec(memory_space=pltpu.SMEM)

    def v(shape, dtype=F32):
        return pltpu.VMEM(shape, dtype)

    scratch = [
        v((atoms, feat), BF16), v((hid + 16, atoms), BF16), v((hid, atoms), BF16),
        v((hid, atoms), BF16), v((hid, atoms), BF16), v((128, atoms), BF16),
        v((8, atoms)), v((1, atoms)),
        v((hid, feat), BF16), v((hid, feat), BF16), v((hid, hid), BF16), v((hid, hid), BF16),
        v((hid, 128)), v((hid, 128)), v((hid, 128)), v((hid, 128)),
        v((atoms // 128, 128)), v((n_graph, code_rows, 128)), v((code_rows, n_graph, 128)),
        v((n_leaf, n_graph, 128)),
        v((8 * n_grp, 128)), v((8 * n_grp, 128)), v((2, 8 * n_grp, 128)), v((8 * n_grp, 128)),
        v((128, 128), jnp.int32),
        v((n_leaf * 8 + 16, 128)), v((n_leaf, 24, 128)), v((24, 128)), v((n_graph, 24, 128)),
        v((8, 128)), v((n_leaf, 8, 128)),
        v((hid + 16, hid)), v((hid, feat)), v((hid, 128)), v((hid, 128)),
        v((hid, hid), BF16), v((hid, feat), BF16),
        v((n_leaf, wrow, hid), BF16), v((n_leaf, wrow, hid), BF16),
        v((2 * wrow, hid), BF16), v((n_graph, 2 * wrow, hid), BF16),
        v((2 * wrow, hid), BF16), v((n_leaf, 2 * wrow, hid), BF16),
        v((8, 128)), v((n_leaf, 8, 128)), v((8, 128)), v((n_graph, 8, 128)),
        pltpu.SemaphoreType.DMA((atoms // chunk,)), pltpu.SemaphoreType.DMA((atoms // chunk,)),
        pltpu.SemaphoreType.DMA((13,)), pltpu.SemaphoreType.DMA((13,)),
    ]
    sds = jax.ShapeDtypeStruct
    outs = pl.pallas_call(
        functools.partial(kernel, n_graph, n_leaf, chunk, n_grp),
        out_shape=(
            sds((atoms, feat), BF16), sds((3, atoms), F32),
            sds((feat, hid), F32), sds((1, hid), F32),
            sds((hid, hid), F32), sds((1, hid), F32), sds((1, hid), F32),
        ),
        in_specs=[any_space, vmem, vmem, vmem, vmem, smem] + [vmem] * 7,
        out_specs=(any_space,) + (vmem,) * 6,
        scratch_shapes=scratch,
        compiler_params=pltpu.CompilerParams(
            collective_id=0, has_side_effects=True, vmem_limit_bytes=60 * 1024 * 1024
        ),
        name="latent_charge",
    )(
        features, positions, energy_weight.reshape(1, atoms), send_slot.reshape(1, atoms),
        tile_slot.reshape(atoms // 128, 128), box_count, list_box, list_image,
        w_in, b_in.reshape(1, hid), w_mid, b_mid.reshape(1, hid), w_out.reshape(1, hid),
    )
    fgrad, pgrad, ing, inb, midg, midb, outg = outs
    return (fgrad, pgrad, ing, inb.reshape(hid), midg, midb.reshape(hid), outg.reshape(hid))


def solution(mesh):
    placed = (
        P(("graph", "leaf"), None),
        P(None, ("graph", "leaf")),
        P(("graph", "leaf")),
        P(("graph", "leaf")),
        P(("graph", "leaf")),
        P("leaf", "graph"),
        P("leaf", None),
        P(None, "leaf", None),
        P(), P(), P(), P(), P(),
    )
    return jax.shard_map(
        body,
        mesh=mesh,
        in_specs=placed,
        out_specs=(P(("graph", "leaf"), None), P(None, ("graph", "leaf")), P(), P(), P(), P(), P()),
        check_vma=False,
    )
```

```python
import functools

import jax
import jax.numpy as jnp
from jax import lax
from jax.experimental import pallas as pl
from jax.experimental.pallas import tpu as pltpu
from jax.sharding import PartitionSpec as P

MESH = pl.DeviceIdType.MESH
F32 = jnp.float32
BF16 = jnp.bfloat16
COUPLING = 0.5
SLOT_DEV = 128
CHUNK = 512
NT = (((1,), (1,)), ((), ()))
NN = (((1,), (0,)), ((), ()))
TN = (((0,), (0,)), ((), ()))


def mm(a, b, dims=NN):
    return lax.dot_general(a, b, dims, preferred_element_type=F32)


def iota(shape, axis):
    return lax.broadcasted_iota(jnp.int32, shape, axis)


def tile_lanes(x, n):
    return jnp.concatenate([x] * (n // x.shape[1]), 1)


def fold_lanes(x):
    parts = [x[:, i : i + 128] for i in range(0, x.shape[1], 128)]
    total = parts[0]
    for part in parts[1:]:
        total = total + part
    return total


def roll(x, shift):
    return pltpu.roll(x, shift % 128, 1)


def shift_x(x):
    first = roll(pltpu.roll(x, 120, 1, stride=1, stride_axis=0), 6)
    col = iota(x.shape, 1) % 8 + 2 - iota(x.shape, 0)
    return jnp.where(col > 7, roll(first, 8), jnp.where(col < 0, roll(first, -8), first))


def shift_y(x, dy):
    if dy == 0:
        return x
    straight = roll(x, -8 * dy)
    row = (iota(x.shape, 1) // 8) % 8 + dy
    return jnp.where((row >= 0) & (row < 8), straight, roll(straight, 64))


def shift_z(slabs, dz):
    if dz % 2 == 0:
        return slabs[dz // 2 + 1]
    low, high = (0, 1) if dz == -1 else (1, 2)
    lower = iota(slabs[1].shape, 1) < 64
    return jnp.where(lower, roll(slabs[low], 64), roll(slabs[high], 64))


def kernel(
    n_graph, n_leaf, chunk, n_grp,
    feat, pos, ew, sslot, tslot, count, lbox, limg, w_in, b_in, w_mid, b_mid, w_out,
    fgrad, pgrad, ing, inb, midg, midb, outg,
    X, A1, SL1, A2, SL2, OB, OD, BLK, U, Q, W1H, W1T, W2TH, W2H, B1, B2, WO,
    CODE, CA, CB, CS, F, G, GN, R, LCODE, MACC, MX, P1, S1, P2, TO, TB,
    ACC, OGACC, IBACC, BOTH, RX, SB, RM, GS, GM, AS, AM, AO,
    BV, BX, BC, BL, BS, BG,
    xsem, osem, ssem, rsem,
):
    g = lax.axis_index("graph")
    l = lax.axis_index("leaf")
    core = lax.rem(g, 2)
    zpos = g // 2
    atoms = X.shape[0]
    hid = SL1.shape[0]
    cap = atoms // (n_graph * n_leaf)
    leaf_bits = n_leaf.bit_length() - 1
    cap_bits = cap.bit_length() - 1
    code_rows = n_leaf * cap // 128
    box_dev = 128
    wrow = hid // n_leaf
    n_z = n_graph // 2
    n_chunks = atoms // chunk
    half_grp = 2 * (n_grp // 5)

    def leaf_peer(o):
        return lax.rem(l + o, n_leaf)

    def send(k, src, dst, device):
        pltpu.make_async_remote_copy(
            src_ref=src, dst_ref=dst, send_sem=ssem.at[k], recv_sem=rsem.at[k],
            device_id=device, device_id_type=MESH,
        ).start()

    def to_leaf(k, src_of, dst):
        @pl.loop(1, n_leaf)
        def _(o):
            peer = leaf_peer(o)
            send(k, src_of(peer), dst, (g, peer))

    def to_graph(k, src_of, dst):
        @pl.loop(1, n_graph)
        def _(o):
            peer = lax.rem(g + o, n_graph)
            send(k, src_of(peer), dst, (peer, l))

    def to_z(k, src, dst):
        @pl.loop(1, n_z)
        def _(o):
            send(k, src, dst, (lax.rem(g + 2 * o, n_graph), l))

    def to_core(k, src, dst):
        send(k, src, dst, (g + 1 - 2 * core, l))

    def wait_on(sem, view):
        pltpu.make_async_copy(view, view, sem).wait()

    bar = pltpu.get_barrier_semaphore()

    @pl.loop(1, n_leaf)
    def _(o):
        pl.semaphore_signal(bar, inc=1, device_id=(g, leaf_peer(o)), device_id_type=MESH)

    @pl.loop(1, n_graph)
    def _(o):
        pl.semaphore_signal(
            bar, inc=1, device_id=(lax.rem(g + o, n_graph), l), device_id_type=MESH
        )

    def feat_copy(c):
        rows = pl.ds(c * chunk, chunk)
        return pltpu.make_async_copy(feat.at[rows], X.at[rows], xsem.at[c])

    @pl.loop(0, n_chunks)
    def _(c):
        feat_copy(c).start()

    slot = tslot[...]
    box = slot >> 7

    def count_step(b, cnt):
        return jnp.where(box == b, count[0, b], cnt)

    cnt = lax.fori_loop(0, box_dev, count_step, jnp.zeros_like(slot), unroll=8)
    CODE[...] = jnp.where((slot & (SLOT_DEV - 1)) < cnt, box, -1).astype(F32)
    CA[g] = CODE[pl.ds(pl.multiple_of(g * code_rows, code_rows), code_rows), :]

    w1 = w_in[...].astype(F32).T
    W1T[...] = w1.astype(BF16)
    W1H[...] = (0.5 * w1).astype(BF16)
    w2 = w_mid[...].astype(F32)
    W2H[...] = (0.5 * w2).astype(BF16)
    W2TH[...] = (0.5 * w2.T).astype(BF16)

    def column(row):
        return jnp.broadcast_to(row, (128, row.shape[1])).T

    B1[...] = column(0.5 * b_in[...])
    B2[...] = column(0.5 * b_mid[...])
    for i in range(hid // 128):
        WO[128 * i : 128 * i + 128, :] = column(w_out[i : i + 1, :].astype(F32))
    A1[hid:, :] = jnp.ones((A1.shape[0] - hid, atoms), BF16)
    U[...] = jnp.ones_like(U)
    U[1:4, :] = pos[...]
    U[5:8, :] = pos[...]

    own = l * box_dev + iota((lbox.shape[0], box_dev), 1)
    src = lbox[...]
    dims = (8, 8, n_leaf * box_dev // 64)
    dx, dy, dz = [
        coord(src) + limg[i] * dims[i] - coord(own)
        for i, coord in enumerate([lambda b: b & 7, lambda b: (b >> 3) & 7, lambda b: b >> 6])
    ]
    LCODE[...] = ((dz + 2) * 5 + dy + 2) * 8 + 2 - dx
    sub = iota((8, 128), 0)

    def mask_step(k, masks):
        row = LCODE[pl.ds(k, 1), :] - sub
        return tuple(m + jnp.where(row == 8 * i, 1.0, 0.0) for i, m in enumerate(masks))

    masks = lax.fori_loop(
        0, lbox.shape[0], mask_step, tuple(jnp.zeros((8, 128), F32) for _ in range(n_grp)), unroll=4
    )
    G[...] = jnp.zeros_like(G)
    for i in range(n_grp):
        F[8 * i : 8 * i + 8, :] = masks[i]
    for i in range(n_grp):
        for j in range(5):
            other = 8 * (n_grp - 1 - i) + 4 - j
            G[8 * i + j : 8 * i + j + 1, :] = F[other : other + 1, :]

    def scale_row(cols):
        return (0.5 * COUPLING) * ew[:, cols]

    def one_hot(index, n):
        return jnp.where(iota((n, chunk), 0) == index, 1.0, 0.0).astype(BF16)

    def head(c):
        feat_copy(c).wait()
        at = pl.ds(pl.multiple_of(c * chunk, chunk), chunk)
        h = mm(W1H[...], X[at, :], NT) + tile_lanes(B1[...], chunk)
        t = jnp.tanh(h)
        a = (h + h * t).astype(BF16)
        t = t.astype(BF16)
        A1[:hid, at] = a
        SL1[:, at] = (1 + a) + t * (1 - a)
        h = mm(W2TH[...], a) + tile_lanes(B2[...], chunk)
        t = jnp.tanh(h)
        wo = tile_lanes(WO[...], chunk)
        a = h + h * t
        Q[:, at] = jnp.sum(a * wo, 0, keepdims=True)
        a = a.astype(BF16)
        A2[:, at] = a
        t = t.astype(BF16)
        SL2[:, at] = ((1 + a) + t * (1 - a)) * (0.5 * wo).astype(BF16)

    def before_place(c):
        cols = pl.ds(pl.multiple_of(c * chunk, chunk), chunk)
        s = sslot[:, cols]
        src_leaf = (s >> cap_bits) & (n_leaf - 1)
        row = src_leaf * n_graph + (s >> (cap_bits + leaf_bits))
        OD[:, cols] = one_hot(row, n_leaf * n_graph)
        q = Q[:, cols]
        sub = iota((8, chunk), 0)
        vals = U[:, cols] * jnp.where(sub < 4, q, scale_row(cols) * q)
        hi = vals.astype(BF16).astype(F32)
        lo = vals - hi
        masks = [src_leaf == i for i in range(n_leaf)]
        blocks = [jnp.where(m, hi, 0.0) for m in masks] + [jnp.where(m, lo, 0.0) for m in masks]
        BLK[:, cols] = jnp.concatenate(blocks, 0).astype(BF16)

    def before_grad(c):
        cols = pl.ds(pl.multiple_of(c * chunk, chunk), chunk)
        slope = mm(W2H[...], SL2[:, cols]) * SL1[:, cols].astype(F32)
        SL1[:, cols] = slope.astype(BF16)

    def first_leg():
        pl.semaphore_wait(bar, n_leaf + n_graph - 2)
        to_graph(
            0,
            lambda peer: CODE.at[pl.ds(pl.multiple_of(peer * code_rows, code_rows), code_rows)],
            CA.at[g],
        )
        rows = 8 * half_grp
        send(2, G.at[pl.ds(0, rows)], GN.at[0], (g, leaf_peer(1)))
        send(3, G.at[pl.ds(8 * n_grp - rows, rows)], GN.at[1], (g, leaf_peer(n_leaf - 1)))

    half = 128 // cap

    def second_leg():
        wait_on(rsem.at[0], CA.at[pl.ds(0, n_graph - 1)])
        flat = CA[...]
        for r in range(code_rows):
            CB[r] = flat[:, r, :]
        CS[l] = CB[l // half]
        to_leaf(1, lambda peer: CB.at[peer // half], CS.at[l])

    leg_at = (n_chunks * 4 // 16, n_chunks * 10 // 16)

    @pl.loop(0, n_chunks)
    def _(c):
        pl.when(c == leg_at[0])(first_leg)
        pl.when(c == leg_at[1])(second_leg)
        head(c)

    pl.loop(0, n_chunks)(before_place)

    wait_on(rsem.at[1], CS.at[pl.ds(0, n_leaf - 1)])
    codes = CS[...].reshape(n_leaf * n_graph, 128).T
    mine = codes[:cap]
    for i in range(1, half):
        mine = jnp.where(lax.rem(l, half) == i, codes[i * cap : (i + 1) * cap], mine)
    mine = mine.astype(BF16)
    MACC[...] = jnp.zeros_like(MACC)

    def place(c):
        cols = pl.ds(pl.multiple_of(c * chunk, chunk), chunk)
        picked = mm(mine, OD[:, cols])
        in_row = iota((cap, chunk), 0) == (sslot[:, cols] & (cap - 1))
        atom_box = jnp.sum(jnp.where(in_row, picked, 0.0), 0, keepdims=True)
        ob = one_hot(atom_box.astype(jnp.int32), box_dev)
        OB[:, cols] = ob
        MACC[...] += mm(BLK[:, cols], ob, NT)

    pl.loop(0, n_chunks)(place)

    rows = n_leaf * 8
    part = MACC[:rows, :] + MACC[rows:, :]
    MX[8 : rows + 8, :] = part
    MX[:8, :] = part[rows - 8 :]
    MX[rows + 8 :, :] = part[:8]
    P1[l] = MX[pl.ds(pl.multiple_of(l * 8, 8), 24), :]
    to_leaf(4, lambda peer: MX.at[pl.ds(pl.multiple_of(peer * 8, 8), 24)], P1.at[l])

    wait_on(rsem.at[2], GN.at[0])
    wait_on(rsem.at[3], GN.at[1])
    for i in range(n_grp):
        at = pl.ds(8 * i, 8)
        slabs = [None, shift_x(G[at, :]), None]
        if i < half_grp:
            slabs[0] = shift_x(GN[0, at, :])
        if i >= n_grp - half_grp:
            slabs[2] = shift_x(GN[1, pl.ds(8 * (i - n_grp + half_grp), 8), :])
        R[at, :] = shift_y(shift_z(slabs, i // 5 - 2), i % 5 - 2)
    ACC[...] = jnp.zeros_like(ACC)
    OGACC[...] = jnp.zeros_like(OGACC)
    IBACC[...] = jnp.zeros_like(IBACC)
    cut = [n_chunks * i // 4 for i in range(5)]
    pl.loop(cut[0], cut[2])(before_grad)

    wait_on(rsem.at[4], P1.at[pl.ds(0, n_leaf - 1)])
    total = jnp.sum(P1[...], 0)
    S1[...] = total
    P2[g] = total
    to_graph(5, lambda peer: S1, P2.at[g])
    pl.loop(cut[2], cut[3])(before_grad)
    wait_on(rsem.at[5], P2.at[pl.ds(0, n_graph - 1)])
    total = jnp.sum(P2[...], 0)

    shifted = []
    for ch in range(8):
        slabs = [
            shift_x(jnp.broadcast_to(total[8 * s + ch : 8 * s + ch + 1], (8, 128))) for s in range(3)
        ]
        shifted.append([shift_z(slabs, d) for d in range(-2, 3)])
    off_x = (2 - iota((8, 128), 0)).astype(F32)
    sums = [jnp.zeros((8, 128), F32) for _ in range(8)]
    for i in range(n_grp):
        off_z, off_y = i // 5 - 2, i % 5 - 2
        dist = jnp.maximum(off_x * off_x + float(off_z * off_z + off_y * off_y), 1.0)
        inv = lax.rsqrt(dist)
        cube = inv * inv * inv
        three = 3.0 * inv * inv
        for base, mask in ((0, F), (4, R)):
            m = mask[8 * i : 8 * i + 8, :]
            q0, q1, q2, q3 = [
                m * shift_y(shifted[base + j][off_z + 2], off_y) for j in range(4)
            ]
            proj = off_x * q1 + float(off_y) * q2 + float(off_z) * q3
            sums[base] += q0 * inv - proj * cube
            radial = q0 - three * proj
            sums[base + 1] += (radial * off_x + q1) * cube
            sums[base + 2] += (radial * float(off_y) + q2) * cube
            sums[base + 3] += (radial * float(off_z) + q3) * cube
    for j in range(8):
        TO[j : j + 1, :] = jnp.sum(sums[j], 0, keepdims=True)
    TB[l] = TO[...]
    to_leaf(6, lambda peer: TO, TB.at[l])
    pl.loop(cut[3], cut[4])(before_grad)
    wait_on(rsem.at[6], TB.at[pl.ds(0, n_leaf - 1)])
    table = TB[...].reshape(rows, 128)
    hi = table.astype(BF16)
    table = jnp.concatenate([hi, (table - hi.astype(F32)).astype(BF16)], 0)

    def backward(c):
        cols = pl.ds(pl.multiple_of(c * chunk, chunk), chunk)
        src_leaf = (sslot[:, cols] >> cap_bits) & (n_leaf - 1)
        got = mm(table, OB[:, cols])
        got = got[:rows] + got[rows:]
        field = jnp.zeros((8, chunk), F32)
        for i in range(n_leaf):
            field += jnp.where(src_leaf == i, got[8 * i : 8 * i + 8], 0.0)
        sub = iota((8, chunk), 0)
        terms = field * U[:, cols]
        q = Q[:, cols]
        w = scale_row(cols)
        grad = jnp.sum(terms * jnp.where(sub < 4, w, 1.0), 0, keepdims=True)
        force = field * jnp.where(sub < 4, w * q, q)
        force = force + pltpu.roll(force, 4, 0)
        pgrad[:, cols] = force[1:4]
        grad = jnp.broadcast_to(grad, (16, chunk)).astype(BF16)[None]

        def scaled(ref):
            x = ref[:, cols].reshape(hid // 16, 16, chunk) * grad
            return x.reshape(hid, chunk)

        ACC[0] += mm(A1[:, cols], scaled(SL2), NT)
        slope = scaled(SL1)
        SL1[:, cols] = slope
        ACC[1, :hid, :] += mm(slope, X[cols, :])
        IBACC[...] += fold_lanes(slope.astype(F32))
        OGACC[...] += fold_lanes(scaled(A2).astype(F32))

    pl.loop(0, n_chunks)(backward)

    BOTH[...] = ACC[:, :hid, :].astype(BF16)
    to_core(7, BOTH.at[1 - core], RX)

    def to_row(columns):
        return jnp.sum(columns.T, 0, keepdims=True)

    BV[...] = jnp.zeros_like(BV)
    vectors = (ACC[0, hid : hid + 1, :], to_row(OGACC[...]), to_row(IBACC[...]))
    for i, vector in enumerate(vectors):
        for j in range(hid // 128):
            at = 2 * i + j
            BV[at : at + 1, :] = vector[:, 128 * j : 128 * j + 128]
    BX[core] = BV[...]
    to_core(8, BV, BX.at[core])
    wait_on(rsem.at[7], RX)
    SB[...] = (ACC[core, :hid, :] + RX[...].astype(F32)).astype(BF16)
    RM[l] = SB[pl.ds(pl.multiple_of(l * wrow, wrow), wrow), :]
    to_leaf(9, lambda peer: SB.at[pl.ds(pl.multiple_of(peer * wrow, wrow), wrow)], RM.at[l])
    wait_on(rsem.at[8], BV)
    BC[...] = BX[0] + BX[1]
    BL[l] = BC[...]
    to_leaf(10, lambda peer: BC, BL.at[l])

    def out_copy(c):
        rows = pl.ds(c * chunk, chunk)
        return pltpu.make_async_copy(X.at[rows], fgrad.at[rows], osem.at[c])

    def backward_row(c):
        at = pl.ds(pl.multiple_of(c * chunk, chunk), chunk)
        X[at, :] = mm(SL1[:, at], W1T[...], TN).astype(BF16)
        out_copy(c).start()

    def sum_leaf():
        wait_on(rsem.at[9], RM.at[pl.ds(0, n_leaf - 1)])
        wait_on(rsem.at[10], BL.at[pl.ds(0, n_leaf - 1)])
        GS[...] = jnp.sum(RM[...].astype(F32), 0).astype(BF16)
        GM[zpos] = GS[...]
        to_z(11, GS, GM.at[zpos])
        BS[...] = jnp.sum(BL[...], 0)
        BG[zpos] = BS[...]
        to_z(12, BS, BG.at[zpos])

    @pl.loop(0, n_chunks)
    def _(c):
        backward_row(c)

    sum_leaf()
    wait_on(rsem.at[11], GM.at[pl.ds(0, n_z - 1)])
    AS[...] = jnp.sum(GM[...].astype(F32), 0).astype(BF16)
    AM[l] = AS[...]
    to_leaf(13, lambda peer: AS, AM.at[l])
    wait_on(rsem.at[12], BG.at[pl.ds(0, n_z - 1)])
    bias = jnp.sum(BG[...], 0)
    for i, out in enumerate((midb, outg, inb)):
        for j in range(hid // 128):
            out[:, 128 * j : 128 * j + 128] = bias[2 * i + j : 2 * i + j + 1]
    wait_on(rsem.at[13], AM.at[pl.ds(0, n_leaf - 1)])
    to_core(14, AM, AO)
    mine = AM[...].astype(F32).reshape(hid, hid)
    wait_on(rsem.at[14], AO)
    other = AO[...].astype(F32).reshape(hid, hid)
    midg[...] = jnp.where(core == 0, mine, other)
    ing[...] = jnp.where(core == 0, other, mine).T

    leaf_sent = pl.ds(0, n_leaf - 1)
    graph_sent = pl.ds(0, n_graph - 1)
    z_sent = pl.ds(0, n_z - 1)
    for k, view in enumerate(
        (
            CA.at[graph_sent], CS.at[leaf_sent], GN.at[0], GN.at[1], P1.at[leaf_sent],
            P2.at[graph_sent], TB.at[leaf_sent], RX, BV, RM.at[leaf_sent], BL.at[leaf_sent],
            GM.at[z_sent], BG.at[z_sent], AM.at[leaf_sent], AO,
        )
    ):
        wait_on(ssem.at[k], view)

    @pl.loop(0, n_chunks)
    def _(c):
        out_copy(c).wait()


def copy_out(pieces, *refs):
    n = (len(refs) - 2) // 3
    legs = []
    sems = refs[-2:]
    for src, dst, held in zip(refs[:n], refs[n : 2 * n], refs[2 * n : 3 * n]):
        parts = pieces if src.shape[0] > 1024 else 1
        rows = src.shape[0] // parts
        for i in range(parts):
            at = pl.ds(i * rows, rows)
            k = len(legs)
            legs.append(
                (
                    pltpu.make_async_copy(src.at[at], held.at[at], sems[0].at[k]),
                    pltpu.make_async_copy(held.at[at], dst.at[at], sems[1].at[k]),
                )
            )
    for load, _ in legs:
        load.start()
    for load, store in legs:
        load.wait()
        store.start()
    for _, store in legs:
        store.wait()


def body(
    features, positions, energy_weight, send_slot, tile_slot, box_count, list_box, list_image,
    w_in, b_in, w_mid, b_mid, w_out,
):
    n_graph, n_leaf = lax.axis_size("graph"), lax.axis_size("leaf")
    atoms, feat = features.shape
    hid = w_in.shape[1]
    chunk = min(CHUNK, atoms // 4)
    n_grp = 25
    n_z = n_graph // 2
    code_rows = n_leaf * (atoms // (n_graph * n_leaf)) // 128
    wrow = hid // n_leaf
    vmem = pl.BlockSpec(memory_space=pltpu.VMEM)
    any_space = pl.BlockSpec(memory_space=pl.ANY)
    smem = pl.BlockSpec(memory_space=pltpu.SMEM)

    def v(shape, dtype=F32):
        return pltpu.VMEM(shape, dtype)

    scratch = [
        v((atoms, feat), BF16), v((hid + 16, atoms), BF16), v((hid, atoms), BF16),
        v((hid, atoms), BF16), v((hid, atoms), BF16), v((128, atoms), BF16),
        v((n_leaf * n_graph, atoms), BF16), v((n_leaf * 16, atoms), BF16),
        v((8, atoms)), v((1, atoms)),
        v((hid, feat), BF16), v((hid, feat), BF16), v((hid, hid), BF16), v((hid, hid), BF16),
        v((hid, 128)), v((hid, 128)), v((hid, 128)),
        v((atoms // 128, 128)), v((n_graph, code_rows, 128)), v((code_rows, n_graph, 128)),
        v((n_leaf, n_graph, 128)),
        v((8 * n_grp, 128)), v((8 * n_grp, 128)), v((2, 80, 128)), v((8 * n_grp, 128)),
        v((list_box.shape[1], 128), jnp.int32),
        v((n_leaf * 16, 128)),
        v((n_leaf * 8 + 16, 128)), v((n_leaf, 24, 128)), v((24, 128)), v((n_graph, 24, 128)),
        v((8, 128)), v((n_leaf, 8, 128)),
        v((2, hid + 16, hid)), v((hid, 128)), v((hid, 128)),
        v((2, hid, hid), BF16), v((hid, hid), BF16), v((hid, hid), BF16),
        v((n_leaf, wrow, hid), BF16), v((wrow, hid), BF16), v((n_z, wrow, hid), BF16),
        v((wrow, hid), BF16), v((n_leaf, wrow, hid), BF16), v((n_leaf, wrow, hid), BF16),
        v((8, 128)), v((2, 8, 128)), v((8, 128)), v((n_leaf, 8, 128)), v((8, 128)),
        v((n_z, 8, 128)),
        pltpu.SemaphoreType.DMA((atoms // chunk,)), pltpu.SemaphoreType.DMA((atoms // chunk,)),
        pltpu.SemaphoreType.DMA((15,)), pltpu.SemaphoreType.DMA((15,)),
    ]
    sds = jax.ShapeDtypeStruct
    shapes = (
        sds((atoms, feat), BF16), sds((3, atoms), F32),
        sds((feat, hid), F32), sds((1, hid), F32),
        sds((hid, hid), F32), sds((1, hid), F32), sds((1, hid), F32),
    )
    outs = pl.pallas_call(
        functools.partial(kernel, n_graph, n_leaf, chunk, n_grp),
        out_shape=shapes,
        in_specs=[any_space, vmem, vmem, vmem, vmem, smem] + [vmem] * 7,
        out_specs=(any_space,) + (vmem,) * 6,
        scratch_shapes=scratch,
        compiler_params=pltpu.CompilerParams(
            collective_id=0, has_side_effects=True, vmem_limit_bytes=56 * 1024 * 1024
        ),
        name="latent_charge",
    )(
        features, positions, energy_weight.reshape(1, atoms), send_slot.reshape(1, atoms),
        tile_slot.reshape(atoms // 128, 128), box_count.reshape(1, -1), list_box.T,
        list_image.transpose(0, 2, 1), w_in, b_in.reshape(1, hid), w_mid, b_mid.reshape(1, hid),
        w_out.reshape(hid // 128, 128),
    )
    pieces = 8
    legs = pieces + len(shapes)
    outs = pl.pallas_call(
        functools.partial(copy_out, pieces),
        out_shape=shapes,
        in_specs=[any_space] * len(shapes),
        out_specs=(any_space,) * len(shapes),
        scratch_shapes=[v(x.shape, x.dtype) for x in shapes]
        + [pltpu.SemaphoreType.DMA((legs,)), pltpu.SemaphoreType.DMA((legs,))],
        compiler_params=pltpu.CompilerParams(vmem_limit_bytes=56 * 1024 * 1024),
        name="results",
    )(*outs)
    fgrad, pgrad, ing, inb, midg, midb, outg = outs
    return (fgrad, pgrad, ing, inb.reshape(hid), midg, midb.reshape(hid), outg.reshape(hid))


def solution(mesh):
    placed = (
        P(("graph", "leaf"), None),
        P(None, ("graph", "leaf")),
        P(("graph", "leaf")),
        P(("graph", "leaf")),
        P(("graph", "leaf")),
        P("leaf", "graph"),
        P("leaf", None),
        P(None, "leaf", None),
        P(), P(), P(), P(), P(),
    )
    return jax.shard_map(
        body,
        mesh=mesh,
        in_specs=placed,
        out_specs=(P(("graph", "leaf"), None), P(None, ("graph", "leaf")), P(), P(), P(), P(), P()),
        check_vma=False,
    )
```

```python
import functools

import jax
import jax.numpy as jnp
from jax import lax
from jax.experimental import pallas as pl
from jax.experimental.pallas import tpu as pltpu
from jax.sharding import PartitionSpec as P

MESH = pl.DeviceIdType.MESH
F32 = jnp.float32
BF16 = jnp.bfloat16
COUPLING = 0.5
SLOT_DEV = 128
HEAD_CHUNK = 1024
CHUNK = 2048
NT = (((1,), (1,)), ((), ()))
NN = (((1,), (0,)), ((), ()))
TN = (((0,), (0,)), ((), ()))


def mm(a, b, dims=NN):
    return lax.dot_general(a, b, dims, preferred_element_type=F32)


def iota(shape, axis):
    return lax.broadcasted_iota(jnp.int32, shape, axis)


def tile_lanes(x, n):
    return jnp.concatenate([x] * (n // x.shape[1]), 1)


def fold_lanes(x):
    parts = [x[:, i : i + 128] for i in range(0, x.shape[1], 128)]
    total = parts[0]
    for part in parts[1:]:
        total = total + part
    return total


def roll(x, shift):
    return pltpu.roll(x, shift % 128, 1)


def shift_x(x):
    first = roll(pltpu.roll(x, 120, 1, stride=1, stride_axis=0), 6)
    col = iota(x.shape, 1) % 8 + 2 - iota(x.shape, 0)
    return jnp.where(col > 7, roll(first, 8), jnp.where(col < 0, roll(first, -8), first))


def shift_y(x, dy):
    if dy == 0:
        return x
    straight = roll(x, -8 * dy)
    row = (iota(x.shape, 1) // 8) % 8 + dy
    return jnp.where((row >= 0) & (row < 8), straight, roll(straight, 64))


def shift_z(slabs, dz):
    if dz % 2 == 0:
        return slabs[dz // 2 + 1]
    low, high = (0, 1) if dz == -1 else (1, 2)
    lower = iota(slabs[1].shape, 1) < 64
    return jnp.where(lower, roll(slabs[low], 64), roll(slabs[high], 64))


def kernel(
    n_graph, n_leaf, head_chunk, chunk, n_grp,
    feat, *refs,
):
    ins, refs = refs[:12], refs[12:]
    outs, refs = refs[:4], refs[4:]
    (pos, ew, sslot, tslot, count, lbox, limg, w_in, b_in, w_mid, b_mid, w_out), refs = (
        refs[:12], refs[12:],
    )
    fgrad, pgrad, mats, bias_out = outs
    (
    X, A1, SL1, A2, SL2, OB, OD, BLK, U, Q, W1H, W1T, W2TH, W2H, B1, B2, WO,
    CODE, CA, CB, CS, F, G, GN, R, LCODE, MACC, MX, P1, S1, P2, TO, TB,
    ACC, OGACC, IBACC, BOTH, RX, SB, RM, GS, GM, AS, AM, AO,
    BV, BX, BC, BL, BS, BG, BF, GR, FIELD, PG,
    xsem, osem, isem, ssem, rsem,
    ) = refs
    g = lax.axis_index("graph")
    l = lax.axis_index("leaf")
    core = lax.rem(g, 2)
    zpos = g // 2
    atoms = X.shape[0]
    hid = SL1.shape[0]
    cap = atoms // (n_graph * n_leaf)
    leaf_bits = n_leaf.bit_length() - 1
    cap_bits = cap.bit_length() - 1
    code_rows = n_leaf * cap // 128
    box_dev = 128
    wrow = hid // n_leaf
    n_z = n_graph // 2
    n_heads = atoms // head_chunk
    n_chunks = atoms // chunk
    half_grp = 2 * (n_grp // 5)

    def leaf_peer(o):
        return lax.rem(l + o, n_leaf)

    def send(k, src, dst, device):
        pltpu.make_async_remote_copy(
            src_ref=src, dst_ref=dst, send_sem=ssem.at[k], recv_sem=rsem.at[k],
            device_id=device, device_id_type=MESH,
        ).start()

    def to_leaf(k, src_of, dst):
        @pl.loop(1, n_leaf)
        def _(o):
            peer = leaf_peer(o)
            send(k, src_of(peer), dst, (g, peer))

    def to_graph(k, src_of, dst):
        @pl.loop(1, n_graph)
        def _(o):
            peer = lax.rem(g + o, n_graph)
            send(k, src_of(peer), dst, (peer, l))

    def to_z(k, src, dst):
        @pl.loop(1, n_z)
        def _(o):
            send(k, src, dst, (lax.rem(g + 2 * o, n_graph), l))

    def to_core(k, src, dst):
        send(k, src, dst, (g + 1 - 2 * core, l))

    def wait_on(sem, view):
        pltpu.make_async_copy(view, view, sem).wait()

    bar = pltpu.get_barrier_semaphore()

    @pl.loop(1, n_leaf)
    def _(o):
        pl.semaphore_signal(bar, inc=1, device_id=(g, leaf_peer(o)), device_id_type=MESH)

    @pl.loop(1, n_graph)
    def _(o):
        pl.semaphore_signal(
            bar, inc=1, device_id=(lax.rem(g + o, n_graph), l), device_id_type=MESH
        )

    def feat_copy(c):
        rows = pl.ds(c * head_chunk, head_chunk)
        return pltpu.make_async_copy(feat.at[rows], X.at[rows], xsem.at[c])

    fetches = [
        pltpu.make_async_copy(src, dst, isem.at[i])
        for i, (src, dst) in enumerate(
            zip(ins, (pos, ew, sslot, tslot, count, lbox, limg, w_in, b_in, w_mid, b_mid, w_out))
        )
    ]
    for fetch in fetches:
        fetch.start()

    @pl.loop(0, n_heads)
    def _(c):
        feat_copy(c).start()

    for fetch in fetches:
        fetch.wait()

    slot = tslot[...]
    box = slot >> 7

    def count_step(b, cnt):
        return jnp.where(box == b, count[0, b], cnt)

    cnt = lax.fori_loop(0, box_dev, count_step, jnp.zeros_like(slot), unroll=8)
    CODE[...] = jnp.where((slot & (SLOT_DEV - 1)) < cnt, box, -1).astype(F32)
    CA[g] = CODE[pl.ds(pl.multiple_of(g * code_rows, code_rows), code_rows), :]

    w1 = w_in[...].astype(F32).T
    W1T[...] = w1.astype(BF16)
    W1H[...] = (0.5 * w1).astype(BF16)
    w2 = w_mid[...].astype(F32)
    W2H[...] = (0.5 * w2).astype(BF16)
    W2TH[...] = (0.5 * w2.T).astype(BF16)

    def column(row):
        return jnp.broadcast_to(row, (128, row.shape[1])).T

    B1[...] = column(0.5 * b_in[...])
    B2[...] = column(0.5 * b_mid[...])
    for i in range(hid // 128):
        WO[128 * i : 128 * i + 128, :] = column(w_out[i : i + 1, :].astype(F32))
    A1[hid:, :] = jnp.ones((A1.shape[0] - hid, atoms), BF16)
    U[...] = jnp.ones_like(U)
    U[1:4, :] = pos[...]
    U[5:8, :] = pos[...]

    own = l * box_dev + iota((lbox.shape[0], box_dev), 1)
    src = lbox[...]
    dims = (8, 8, n_leaf * box_dev // 64)
    dx, dy, dz = [
        coord(src) + limg[i] * dims[i] - coord(own)
        for i, coord in enumerate([lambda b: b & 7, lambda b: (b >> 3) & 7, lambda b: b >> 6])
    ]
    LCODE[...] = ((dz + 2) * 5 + dy + 2) * 8 + 2 - dx
    sub = iota((8, 128), 0)

    def mask_step(k, masks):
        row = LCODE[pl.ds(k, 1), :] - sub
        return tuple(m + jnp.where(row == 8 * i, 1.0, 0.0) for i, m in enumerate(masks))

    masks = lax.fori_loop(
        0, lbox.shape[0], mask_step, tuple(jnp.zeros((8, 128), F32) for _ in range(n_grp)), unroll=4
    )
    G[...] = jnp.zeros_like(G)
    for i in range(n_grp):
        F[8 * i : 8 * i + 8, :] = masks[i]
    for i in range(n_grp):
        for j in range(5):
            other = 8 * (n_grp - 1 - i) + 4 - j
            G[8 * i + j : 8 * i + j + 1, :] = F[other : other + 1, :]

    def scale_row(cols):
        return (0.5 * COUPLING) * ew[:, cols]

    def one_hot(index, n):
        return jnp.where(iota((n, chunk), 0) == index, 1.0, 0.0).astype(BF16)

    def head(c):
        feat_copy(c).wait()
        at = pl.ds(pl.multiple_of(c * head_chunk, head_chunk), head_chunk)
        h = mm(W1H[...], X[at, :], NT) + tile_lanes(B1[...], head_chunk)
        t = jnp.tanh(h)
        a = (h + h * t).astype(BF16)
        t = t.astype(BF16)
        A1[:hid, at] = a
        SL1[:, at] = (1 + a) + t * (1 - a)
        h = mm(W2TH[...], a) + tile_lanes(B2[...], head_chunk)
        t = jnp.tanh(h)
        wo = tile_lanes(WO[...], head_chunk)
        a = h + h * t
        Q[:, at] = jnp.sum(a * wo, 0, keepdims=True)
        a = a.astype(BF16)
        A2[:, at] = a
        t = t.astype(BF16)
        SL2[:, at] = ((1 + a) + t * (1 - a)) * (0.5 * wo).astype(BF16)

    def before_place(c):
        cols = pl.ds(pl.multiple_of(c * chunk, chunk), chunk)
        s = sslot[:, cols]
        src_leaf = (s >> cap_bits) & (n_leaf - 1)
        row = src_leaf * n_graph + (s >> (cap_bits + leaf_bits))
        OD[:, cols] = one_hot(row, n_leaf * n_graph)
        q = Q[:, cols]
        sub = iota((8, chunk), 0)
        vals = U[:, cols] * jnp.where(sub < 4, q, scale_row(cols) * q)
        hi = vals.astype(BF16).astype(F32)
        lo = vals - hi
        masks = [src_leaf == i for i in range(n_leaf)]
        blocks = [jnp.where(m, hi, 0.0) for m in masks] + [jnp.where(m, lo, 0.0) for m in masks]
        BLK[:, cols] = jnp.concatenate(blocks, 0).astype(BF16)

    def before_grad(c):
        cols = pl.ds(pl.multiple_of(c * chunk, chunk), chunk)
        slope = mm(W2H[...], SL2[:, cols]) * SL1[:, cols].astype(F32)
        SL1[:, cols] = slope.astype(BF16)

    def first_leg():
        pl.semaphore_wait(bar, n_leaf + n_graph - 2)
        to_graph(
            0,
            lambda peer: CODE.at[pl.ds(pl.multiple_of(peer * code_rows, code_rows), code_rows)],
            CA.at[g],
        )
        rows = 8 * half_grp
        send(2, G.at[pl.ds(0, rows)], GN.at[0], (g, leaf_peer(1)))
        send(3, G.at[pl.ds(8 * n_grp - rows, rows)], GN.at[1], (g, leaf_peer(n_leaf - 1)))

    half = 128 // cap

    def second_leg():
        wait_on(rsem.at[0], CA.at[pl.ds(0, n_graph - 1)])
        flat = CA[...]
        for r in range(code_rows):
            CB[r] = flat[:, r, :]
        CS[l] = CB[l // half]
        to_leaf(1, lambda peer: CB.at[peer // half], CS.at[l])

    leg_at = (n_heads * 2 // 16, n_heads * 10 // 16)

    @pl.loop(0, n_heads)
    def _(c):
        pl.when(c == leg_at[0])(first_leg)
        pl.when(c == leg_at[1])(second_leg)
        head(c)

    pl.loop(0, n_chunks)(before_place)

    wait_on(rsem.at[1], CS.at[pl.ds(0, n_leaf - 1)])
    codes = CS[...].reshape(n_leaf * n_graph, 128).T
    mine = codes[:cap]
    for i in range(1, half):
        mine = jnp.where(lax.rem(l, half) == i, codes[i * cap : (i + 1) * cap], mine)
    mine = mine.astype(BF16)
    MACC[...] = jnp.zeros_like(MACC)

    def place(c):
        cols = pl.ds(pl.multiple_of(c * chunk, chunk), chunk)
        picked = mm(mine, OD[:, cols])
        in_row = iota((cap, chunk), 0) == (sslot[:, cols] & (cap - 1))
        atom_box = jnp.sum(jnp.where(in_row, picked, 0.0), 0, keepdims=True)
        ob = one_hot(atom_box.astype(jnp.int32), box_dev)
        OB[:, cols] = ob
        MACC[...] += mm(BLK[:, cols], ob, NT)

    pl.loop(0, n_chunks)(place)

    rows = n_leaf * 8
    part = MACC[:rows, :] + MACC[rows:, :]
    MX[8 : rows + 8, :] = part
    MX[:8, :] = part[rows - 8 :]
    MX[rows + 8 :, :] = part[:8]
    P1[l] = MX[pl.ds(pl.multiple_of(l * 8, 8), 24), :]
    to_leaf(4, lambda peer: MX.at[pl.ds(pl.multiple_of(peer * 8, 8), 24)], P1.at[l])

    wait_on(rsem.at[2], GN.at[0])
    wait_on(rsem.at[3], GN.at[1])
    for i in range(n_grp):
        at = pl.ds(8 * i, 8)
        slabs = [None, shift_x(G[at, :]), None]
        if i < half_grp:
            slabs[0] = shift_x(GN[0, at, :])
        if i >= n_grp - half_grp:
            slabs[2] = shift_x(GN[1, pl.ds(8 * (i - n_grp + half_grp), 8), :])
        R[at, :] = shift_y(shift_z(slabs, i // 5 - 2), i % 5 - 2)
    ACC[...] = jnp.zeros_like(ACC)
    OGACC[...] = jnp.zeros_like(OGACC)
    IBACC[...] = jnp.zeros_like(IBACC)
    cut = [n_chunks * i // 4 for i in range(5)]
    pl.loop(cut[0], cut[2])(before_grad)

    wait_on(rsem.at[4], P1.at[pl.ds(0, n_leaf - 1)])
    total = jnp.sum(P1[...], 0)
    S1[...] = total
    P2[g] = total
    to_graph(5, lambda peer: S1, P2.at[g])
    pl.loop(cut[2], cut[3])(before_grad)
    wait_on(rsem.at[5], P2.at[pl.ds(0, n_graph - 1)])
    total = jnp.sum(P2[...], 0)

    shifted = []
    for ch in range(8):
        slabs = [
            shift_x(jnp.broadcast_to(total[8 * s + ch : 8 * s + ch + 1], (8, 128))) for s in range(3)
        ]
        shifted.append([shift_z(slabs, d) for d in range(-2, 3)])
    off_x = (2 - iota((8, 128), 0)).astype(F32)
    sums = [jnp.zeros((8, 128), F32) for _ in range(8)]
    for i in range(n_grp):
        off_z, off_y = i // 5 - 2, i % 5 - 2
        dist = jnp.maximum(off_x * off_x + float(off_z * off_z + off_y * off_y), 1.0)
        inv = lax.rsqrt(dist)
        cube = inv * inv * inv
        three = 3.0 * inv * inv
        for base, mask in ((0, F), (4, R)):
            m = mask[8 * i : 8 * i + 8, :]
            q0, q1, q2, q3 = [
                m * shift_y(shifted[base + j][off_z + 2], off_y) for j in range(4)
            ]
            proj = off_x * q1 + float(off_y) * q2 + float(off_z) * q3
            sums[base] += q0 * inv - proj * cube
            radial = q0 - three * proj
            sums[base + 1] += (radial * off_x + q1) * cube
            sums[base + 2] += (radial * float(off_y) + q2) * cube
            sums[base + 3] += (radial * float(off_z) + q3) * cube
    for j in range(8):
        TO[j : j + 1, :] = jnp.sum(sums[j], 0, keepdims=True)
    TB[l] = TO[...]
    to_leaf(6, lambda peer: TO, TB.at[l])
    pl.loop(cut[3], cut[4])(before_grad)
    wait_on(rsem.at[6], TB.at[pl.ds(0, n_leaf - 1)])
    table = TB[...].reshape(rows, 128)
    hi = table.astype(BF16)
    table = jnp.concatenate([hi, (table - hi.astype(F32)).astype(BF16)], 0)

    def backward(c):
        cols = pl.ds(pl.multiple_of(c * chunk, chunk), chunk)
        src_leaf = (sslot[:, cols] >> cap_bits) & (n_leaf - 1)
        got = mm(table, OB[:, cols])
        got = got[:rows] + got[rows:]
        field = jnp.zeros((8, chunk), F32)
        for i in range(n_leaf):
            field += jnp.where(src_leaf == i, got[8 * i : 8 * i + 8], 0.0)
        FIELD[:, cols] = field
        sub = iota((8, chunk), 0)
        terms = field * U[:, cols] * jnp.where(sub < 4, scale_row(cols), 1.0)
        grad = jnp.sum(terms, 0, keepdims=True)
        grad = jnp.broadcast_to(grad, (16, chunk)).astype(BF16)
        GR[:, cols] = grad
        grad = grad[None]

        def scaled(ref):
            x = ref[:, cols].reshape(hid // 16, 16, chunk) * grad
            return x.reshape(hid, chunk)

        ACC[0] += mm(A1[:, cols], scaled(SL2), NT)
        slope = scaled(SL1)
        SL1[:, cols] = slope
        ACC[1, :hid, :] += mm(slope, X[cols, :])

    pl.loop(0, n_chunks)(backward)

    BOTH[...] = ACC[:, :hid, :].astype(BF16)
    to_core(7, BOTH.at[1 - core], RX)

    def to_row(columns):
        return jnp.sum(columns.T, 0, keepdims=True)

    wait_on(rsem.at[7], RX)
    SB[...] = (ACC[core, :hid, :] + RX[...].astype(F32)).astype(BF16)
    RM[l] = SB[pl.ds(pl.multiple_of(l * wrow, wrow), wrow), :]
    to_leaf(9, lambda peer: SB.at[pl.ds(pl.multiple_of(peer * wrow, wrow), wrow)], RM.at[l])
    def out_copy(c):
        rows = pl.ds(c * chunk, chunk)
        return pltpu.make_async_copy(X.at[rows], fgrad.at[rows], osem.at[c])

    def backward_row(c):
        at = pl.ds(pl.multiple_of(c * chunk, chunk), chunk)
        X[at, :] = mm(SL1[:, at], W1T[...], TN).astype(BF16)
        out_copy(c).start()
        IBACC[...] += fold_lanes(SL1[:, at].astype(F32))
        og = A2[:, at].reshape(hid // 16, 16, chunk) * GR[:, at][None]
        OGACC[...] += fold_lanes(og.reshape(hid, chunk).astype(F32))
        q = Q[:, at]
        force = FIELD[:, at] * jnp.where(iota((8, chunk), 0) < 4, scale_row(at) * q, q)
        force = force + pltpu.roll(force, 4, 0)
        PG[:, at] = force[1:4]

    pl.loop(0, n_chunks)(backward_row)
    force_copy = pltpu.make_async_copy(PG, pgrad, isem.at[0])
    force_copy.start()
    BV[...] = jnp.zeros_like(BV)
    vectors = (ACC[0, hid : hid + 1, :], to_row(OGACC[...]), to_row(IBACC[...]))
    for i, vector in enumerate(vectors):
        for j in range(hid // 128):
            at = 2 * i + j
            BV[at : at + 1, :] = vector[:, 128 * j : 128 * j + 128]
    BX[core] = BV[...]
    to_core(8, BV, BX.at[core])
    wait_on(rsem.at[8], BV)
    BC[...] = BX[0] + BX[1]
    BL[l] = BC[...]
    to_leaf(10, lambda peer: BC, BL.at[l])

    wait_on(rsem.at[9], RM.at[pl.ds(0, n_leaf - 1)])
    GS[...] = jnp.sum(RM[...].astype(F32), 0).astype(BF16)
    GM[zpos] = GS[...]
    to_z(11, GS, GM.at[zpos])
    wait_on(rsem.at[11], GM.at[pl.ds(0, n_z - 1)])
    AS[...] = jnp.sum(GM[...].astype(F32), 0).astype(BF16)
    AM[l] = AS[...]
    to_leaf(13, lambda peer: AS, AM.at[l])
    wait_on(rsem.at[10], BL.at[pl.ds(0, n_leaf - 1)])
    BS[...] = jnp.sum(BL[...], 0)
    BG[zpos] = BS[...]
    to_z(12, BS, BG.at[zpos])
    wait_on(rsem.at[12], BG.at[pl.ds(0, n_z - 1)])
    BF[...] = jnp.sum(BG[...], 0)
    bias_copy = pltpu.make_async_copy(BF, bias_out, isem.at[1])
    bias_copy.start()
    wait_on(rsem.at[13], AM.at[pl.ds(0, n_leaf - 1)])
    to_core(14, AM, AO)
    mine_copy = pltpu.make_async_copy(AM, mats.at[core], isem.at[2])
    mine_copy.start()

    leaf_sent = pl.ds(0, n_leaf - 1)
    graph_sent = pl.ds(0, n_graph - 1)
    z_sent = pl.ds(0, n_z - 1)
    sent = {
        0: CA.at[graph_sent], 1: CS.at[leaf_sent], 2: GN.at[0], 3: GN.at[1], 4: P1.at[leaf_sent],
        5: P2.at[graph_sent], 6: TB.at[leaf_sent], 7: RX, 8: BV, 9: RM.at[leaf_sent],
        10: BL.at[leaf_sent], 11: GM.at[z_sent], 12: BG.at[z_sent], 13: AM.at[leaf_sent], 14: AO,
    }
    for k, view in sent.items():
        wait_on(ssem.at[k], view)

    @pl.loop(0, n_chunks)
    def _(c):
        out_copy(c).wait()

    force_copy.wait()
    bias_copy.wait()
    wait_on(rsem.at[14], AO)
    other_copy = pltpu.make_async_copy(AO, mats.at[1 - core], isem.at[3])
    other_copy.start()
    mine_copy.wait()
    other_copy.wait()


def finish(
    pieces, fgrad, pgrad, mats, bias, fout, pout, ing, inb, midg, midb, outg,
    FH, PH, MH, BH, IN, MID, IB, MB, OG, lsem, ssem,
):
    rows = FH.shape[0] // pieces
    legs = [
        (fgrad.at[pl.ds(i * rows, rows)], FH.at[pl.ds(i * rows, rows)], fout.at[pl.ds(i * rows, rows)])
        for i in range(pieces)
    ]
    legs.append((pgrad, PH, pout))
    loads = [pltpu.make_async_copy(a, b, lsem.at[i]) for i, (a, b, _) in enumerate(legs)]
    stores = [pltpu.make_async_copy(b, c, ssem.at[i]) for i, (_, b, c) in enumerate(legs)]
    last = len(legs)
    loads.append(pltpu.make_async_copy(mats, MH, lsem.at[last]))
    loads.append(pltpu.make_async_copy(bias, BH, lsem.at[last + 1]))
    for load in loads:
        load.start()
    for load, store in zip(loads, stores):
        load.wait()
        store.start()
    for load in loads[last:]:
        load.wait()
    hid = MID.shape[0]
    MID[...] = MH[0].astype(F32).reshape(hid, hid)
    IN[...] = MH[1].astype(F32).reshape(hid, hid).T
    for i, row in enumerate((MB, OG, IB)):
        for j in range(hid // 128):
            row[:, 128 * j : 128 * j + 128] = BH[2 * i + j : 2 * i + j + 1, :]
    for i, (a, b) in enumerate(((IN, ing), (MID, midg), (IB, inb), (MB, midb), (OG, outg))):
        stores.append(pltpu.make_async_copy(a, b, ssem.at[last + i]))
        stores[-1].start()
    for store in stores:
        store.wait()


def body(
    features, positions, energy_weight, send_slot, tile_slot, box_count, list_box, list_image,
    w_in, b_in, w_mid, b_mid, w_out,
):
    n_graph, n_leaf = lax.axis_size("graph"), lax.axis_size("leaf")
    atoms, feat = features.shape
    hid = w_in.shape[1]
    head_chunk = min(HEAD_CHUNK, atoms // 4)
    chunk = min(CHUNK, atoms // 4)
    n_grp = 25
    n_z = n_graph // 2
    code_rows = n_leaf * (atoms // (n_graph * n_leaf)) // 128
    wrow = hid // n_leaf
    any_space = pl.BlockSpec(memory_space=pl.ANY)

    def v(shape, dtype=F32):
        return pltpu.VMEM(shape, dtype)

    scratch = [
        v((atoms, feat), BF16), v((hid + 16, atoms), BF16), v((hid, atoms), BF16),
        v((hid, atoms), BF16), v((hid, atoms), BF16), v((128, atoms), BF16),
        v((n_leaf * n_graph, atoms), BF16), v((n_leaf * 16, atoms), BF16),
        v((8, atoms)), v((1, atoms)),
        v((hid, feat), BF16), v((hid, feat), BF16), v((hid, hid), BF16), v((hid, hid), BF16),
        v((hid, 128)), v((hid, 128)), v((hid, 128)),
        v((atoms // 128, 128)), v((n_graph, code_rows, 128)), v((code_rows, n_graph, 128)),
        v((n_leaf, n_graph, 128)),
        v((8 * n_grp, 128)), v((8 * n_grp, 128)), v((2, 80, 128)), v((8 * n_grp, 128)),
        v((list_box.shape[1], 128), jnp.int32),
        v((n_leaf * 16, 128)),
        v((n_leaf * 8 + 16, 128)), v((n_leaf, 24, 128)), v((24, 128)), v((n_graph, 24, 128)),
        v((8, 128)), v((n_leaf, 8, 128)),
        v((2, hid + 16, hid)), v((hid, 128)), v((hid, 128)),
        v((2, hid, hid), BF16), v((hid, hid), BF16), v((hid, hid), BF16),
        v((n_leaf, wrow, hid), BF16), v((wrow, hid), BF16), v((n_z, wrow, hid), BF16),
        v((wrow, hid), BF16), v((n_leaf, wrow, hid), BF16), v((n_leaf, wrow, hid), BF16),
        v((8, 128)), v((2, 8, 128)), v((8, 128)), v((n_leaf, 8, 128)), v((8, 128)),
        v((n_z, 8, 128)), v((8, 128)), v((16, atoms), BF16), v((8, atoms)), v((3, atoms)),
        pltpu.SemaphoreType.DMA((atoms // head_chunk,)), pltpu.SemaphoreType.DMA((atoms // chunk,)),
        pltpu.SemaphoreType.DMA((12,)), pltpu.SemaphoreType.DMA((15,)),
        pltpu.SemaphoreType.DMA((15,)),
    ]
    sds = jax.ShapeDtypeStruct
    shapes = (
        sds((atoms, feat), BF16), sds((3, atoms), F32),
        sds((feat, hid), F32), sds((1, hid), F32),
        sds((hid, hid), F32), sds((1, hid), F32), sds((1, hid), F32),
    )
    mids = (
        shapes[0], shapes[1], sds((2, n_leaf, wrow, hid), BF16), sds((8, 128), F32),
    )
    ins = (
        positions, energy_weight.reshape(1, atoms), send_slot.reshape(1, atoms),
        tile_slot.reshape(atoms // 128, 128), box_count.reshape(1, -1), list_box.T,
        list_image.transpose(0, 2, 1), w_in, b_in.reshape(1, hid), w_mid, b_mid.reshape(1, hid),
        w_out.reshape(hid // 128, 128),
    )
    held = [
        (pltpu.SMEM if i == 4 else pltpu.VMEM)(x.shape, x.dtype) for i, x in enumerate(ins)
    ]
    mids = pl.pallas_call(
        functools.partial(kernel, n_graph, n_leaf, head_chunk, chunk, n_grp),
        out_shape=mids,
        in_specs=[any_space] * 13,
        out_specs=(any_space,) * 4,
        scratch_shapes=held + scratch,
        compiler_params=pltpu.CompilerParams(
            collective_id=0, has_side_effects=True, vmem_limit_bytes=56 * 1024 * 1024
        ),
        name="latent_charge",
    )(features, *ins)
    pieces = 4
    outs = pl.pallas_call(
        functools.partial(finish, pieces),
        out_shape=shapes,
        in_specs=[any_space] * 4,
        out_specs=(any_space,) * len(shapes),
        scratch_shapes=[v(x.shape, x.dtype) for x in mids]
        + [v(shapes[i].shape) for i in (2, 4, 3, 5, 6)]
        + [pltpu.SemaphoreType.DMA((pieces + 3,)), pltpu.SemaphoreType.DMA((pieces + 6,))],
        compiler_params=pltpu.CompilerParams(vmem_limit_bytes=56 * 1024 * 1024),
        name="results",
    )(*mids)
    fgrad, pgrad, ing, inb, midg, midb, outg = outs
    return (fgrad, pgrad, ing, inb.reshape(hid), midg, midb.reshape(hid), outg.reshape(hid))


def solution(mesh):
    placed = (
        P(("graph", "leaf"), None),
        P(None, ("graph", "leaf")),
        P(("graph", "leaf")),
        P(("graph", "leaf")),
        P(("graph", "leaf")),
        P("leaf", "graph"),
        P("leaf", None),
        P(None, "leaf", None),
        P(), P(), P(), P(), P(),
    )
    return jax.shard_map(
        body,
        mesh=mesh,
        in_specs=placed,
        out_specs=(P(("graph", "leaf"), None), P(None, ("graph", "leaf")), P(), P(), P(), P(), P()),
        check_vma=False,
    )
```

```python
import functools

import jax
import jax.numpy as jnp
from jax import lax
from jax.experimental import pallas as pl
from jax.experimental.pallas import tpu as pltpu
from jax.sharding import PartitionSpec as P

MESH = pl.DeviceIdType.MESH
F32 = jnp.float32
BF16 = jnp.bfloat16
COUPLING = 0.5
SLOT_DEV = 128
HEAD_CHUNK = 1024
CHUNK = 4096
NT = (((1,), (1,)), ((), ()))
NN = (((1,), (0,)), ((), ()))
TN = (((0,), (0,)), ((), ()))


def mm(a, b, dims=NN):
    return lax.dot_general(a, b, dims, preferred_element_type=F32)


def iota(shape, axis):
    return lax.broadcasted_iota(jnp.int32, shape, axis)


def tile_lanes(x, n):
    return jnp.concatenate([x] * (n // x.shape[1]), 1)


def fold_lanes(x):
    parts = [x[:, i : i + 128] for i in range(0, x.shape[1], 128)]
    total = parts[0]
    for part in parts[1:]:
        total = total + part
    return total


def roll(x, shift):
    return pltpu.roll(x, shift % 128, 1)


def shift_x(x):
    return wrap_x(roll(pltpu.roll(x, 120, 1, stride=1, stride_axis=0), 6))


def wrap_x(first):
    x = first
    col = iota(x.shape, 1) % 8 + 2 - iota(x.shape, 0)
    return jnp.where(col > 7, roll(first, 8), jnp.where(col < 0, roll(first, -8), first))


def shift_y(x, dy):
    if dy == 0:
        return x
    straight = roll(x, -8 * dy)
    row = (iota(x.shape, 1) // 8) % 8 + dy
    return jnp.where((row >= 0) & (row < 8), straight, roll(straight, 64))


def shift_z(slabs, dz):
    if dz % 2 == 0:
        return slabs[dz // 2 + 1]
    low, high = (0, 1) if dz == -1 else (1, 2)
    lower = iota(slabs[low].shape, 1) < 64
    return jnp.where(lower, roll(slabs[low], 64), roll(slabs[high], 64))


def kernel(
    n_graph, n_leaf, head_chunk, chunk, n_grp,
    feat, *refs,
):
    ins, refs = refs[:12], refs[12:]
    outs, refs = refs[:4], refs[4:]
    (pos, ew, sslot, tslot, count, lbox, limg, w_in, b_in, w_mid, b_mid, w_out), refs = (
        refs[:12], refs[12:],
    )
    fgrad, pgrad, mats, bias_out = outs
    (
    X, A1, SL1, A2, SL2, OB, OD, BLK, U, Q, W1H, W1T, W2TH, W2H, B1, B2, WO, WOH,
    CODE, CA, CB, CS, F, G, GN, R, LCODE, LN, MACC, MX, P1, TO, TX, TC, TB,
    ACC, OGACC, IBACC, BOTH, RX, SB, RM, GS, GM, AS, AM, AO,
    BV, BX, BC, BL, BS, BG, BF, GR, FIELD, PG,
    xsem, osem, isem, ssem, rsem,
    ) = refs
    g = lax.axis_index("graph")
    l = lax.axis_index("leaf")
    core = lax.rem(g, 2)
    zpos = g // 2
    atoms = X.shape[0]
    hid = SL1.shape[0]
    cap = atoms // (n_graph * n_leaf)
    leaf_bits = n_leaf.bit_length() - 1
    cap_bits = cap.bit_length() - 1
    code_rows = n_leaf * cap // 128
    box_dev = 128
    wrow = hid // n_leaf
    n_z = n_graph // 2
    n_heads = atoms // head_chunk
    n_chunks = atoms // chunk

    def leaf_peer(o):
        return lax.rem(l + o, n_leaf)

    def send(k, src, dst, device):
        pltpu.make_async_remote_copy(
            src_ref=src, dst_ref=dst, send_sem=ssem.at[k], recv_sem=rsem.at[k],
            device_id=device, device_id_type=MESH,
        ).start()

    def to_leaf(k, src_of, dst):
        @pl.loop(1, n_leaf)
        def _(o):
            peer = leaf_peer(o)
            send(k, src_of(peer), dst, (g, peer))

    def to_graph(k, src_of, dst):
        @pl.loop(1, n_graph)
        def _(o):
            peer = lax.rem(g + o, n_graph)
            send(k, src_of(peer), dst, (peer, l))

    def to_z(k, src, dst):
        @pl.loop(1, n_z)
        def _(o):
            send(k, src, dst, (lax.rem(g + 2 * o, n_graph), l))

    def to_chips(k, src, dst):
        mine = zpos * n_leaf + l

        @pl.loop(1, n_z * n_leaf)
        def _(o):
            chip = lax.rem(mine + o, n_z * n_leaf)
            send(k, src, dst, (2 * (chip // n_leaf) + core, lax.rem(chip, n_leaf)))

    def to_core(k, src, dst):
        send(k, src, dst, (g + 1 - 2 * core, l))

    def wait_on(sem, view):
        pltpu.make_async_copy(view, view, sem).wait()

    bar = pltpu.get_barrier_semaphore()

    @pl.loop(1, n_leaf)
    def _(o):
        pl.semaphore_signal(bar, inc=1, device_id=(g, leaf_peer(o)), device_id_type=MESH)

    @pl.loop(1, n_graph)
    def _(o):
        pl.semaphore_signal(
            bar, inc=1, device_id=(lax.rem(g + o, n_graph), l), device_id_type=MESH
        )

    def feat_copy(c):
        rows = pl.ds(c * head_chunk, head_chunk)
        return pltpu.make_async_copy(feat.at[rows], X.at[rows], xsem.at[c])

    fetches = [
        pltpu.make_async_copy(src, dst, isem.at[i])
        for i, (src, dst) in enumerate(
            zip(ins, (pos, ew, sslot, tslot, count, lbox, limg, w_in, b_in, w_mid, b_mid, w_out))
        )
    ]
    for fetch in fetches:
        fetch.start()

    @pl.loop(0, n_heads)
    def _(c):
        feat_copy(c).start()

    for fetch in fetches:
        fetch.wait()

    slot = tslot[...]
    box = slot >> 7

    def count_step(b, cnt):
        return jnp.where(box == b, count[0, b], cnt)

    cnt = lax.fori_loop(0, box_dev, count_step, jnp.zeros_like(slot), unroll=8)
    CODE[...] = jnp.where((slot & (SLOT_DEV - 1)) < cnt, box, -1).astype(F32)
    CA[g] = CODE[pl.ds(pl.multiple_of(g * code_rows, code_rows), code_rows), :]

    w1 = w_in[...].astype(F32).T
    W1T[...] = w1.astype(BF16)
    W1H[...] = (0.5 * w1).astype(BF16)
    w2 = w_mid[...].astype(F32)
    W2H[...] = (0.5 * w2).astype(BF16)
    W2TH[...] = (0.5 * w2.T).astype(BF16)

    def column(row):
        return jnp.broadcast_to(row, (128, row.shape[1])).T

    B1[...] = column(0.5 * b_in[...])
    B2[...] = column(0.5 * b_mid[...])
    for i in range(hid // 128):
        wo = column(w_out[i : i + 1, :].astype(F32))
        WO[128 * i : 128 * i + 128, :] = wo
        WOH[128 * i : 128 * i + 128, :] = 0.5 * wo
    A1[hid:, :] = jnp.ones((A1.shape[0] - hid, atoms), BF16)
    U[...] = jnp.ones_like(U)
    U[1:4, :] = pos[...]
    U[5:8, :] = pos[...]

    own = l * box_dev + iota((lbox.shape[0], box_dev), 1)
    src = lbox[...]
    dims = (8, 8, n_leaf * box_dev // 64)
    dx, dy, dz = [
        coord(src) + limg[i] * dims[i] - coord(own)
        for i, coord in enumerate([lambda b: b & 7, lambda b: (b >> 3) & 7, lambda b: b >> 6])
    ]
    LCODE[...] = ((dz + 2) * 5 + dy + 2) * 8 + 2 - dx

    def scale_row(cols):
        return (0.5 * COUPLING) * ew[:, cols]

    def one_hot(index, n):
        return jnp.where(iota((n, chunk), 0) == index, 1.0, 0.0).astype(BF16)

    def head(c):
        feat_copy(c).wait()
        at = pl.ds(pl.multiple_of(c * head_chunk, head_chunk), head_chunk)
        h = mm(W1H[...], X[at, :], NT) + tile_lanes(B1[...], head_chunk)
        t = jnp.tanh(h)
        a = (h + h * t).astype(BF16)
        t = t.astype(BF16)
        A1[:hid, at] = a
        SL1[:, at] = (1 + a) + t * (1 - a)
        h = mm(W2TH[...], a) + tile_lanes(B2[...], head_chunk)
        t = jnp.tanh(h)
        wo = tile_lanes(WO[...], head_chunk)
        a = h + h * t
        Q[:, at] = jnp.sum(a * wo, 0, keepdims=True)
        A2[:, at] = a.astype(BF16)
        half_wo = tile_lanes(WOH[...], head_chunk)
        SL2[:, at] = (((1.0 + a) + t * (1.0 - a)) * half_wo).astype(BF16)

    def before_place(c):
        cols = pl.ds(pl.multiple_of(c * chunk, chunk), chunk)
        s = sslot[:, cols]
        src_leaf = (s >> cap_bits) & (n_leaf - 1)
        row = src_leaf * n_graph + (s >> (cap_bits + leaf_bits))
        row = row + ((s >> (cap_bits - 1)) & 1) * (n_leaf * n_graph)
        OD[:, cols] = one_hot(row, 2 * n_leaf * n_graph)
        q = Q[:, cols]
        sub = iota((8, chunk), 0)
        vals = U[:, cols] * jnp.where(sub < 4, q, scale_row(cols) * q)
        blocks = [jnp.where(src_leaf == i, vals, 0.0) for i in range(n_leaf)]
        BLK[:, cols] = jnp.concatenate(blocks, 0).astype(BF16)

    def before_grad(c):
        cols = pl.ds(pl.multiple_of(c * chunk, chunk), chunk)
        slope = mm(W2H[...], SL2[:, cols]) * SL1[:, cols].astype(F32)
        SL1[:, cols] = slope.astype(BF16)

    def first_leg():
        pl.semaphore_wait(bar, n_leaf + n_graph - 2)
        to_graph(
            0,
            lambda peer: CODE.at[pl.ds(pl.multiple_of(peer * code_rows, code_rows), code_rows)],
            CA.at[g],
        )
        send(2, LCODE, LN.at[0], (g, leaf_peer(1)))
        send(3, LCODE, LN.at[1], (g, leaf_peer(n_leaf - 1)))

    half = 128 // cap

    def second_leg():
        wait_on(rsem.at[0], CA.at[pl.ds(0, n_graph - 1)])
        flat = CA[...]
        for r in range(code_rows):
            CB[r] = flat[:, r, :]
        CS[l] = CB[l // half]
        to_leaf(1, lambda peer: CB.at[peer // half], CS.at[l])

    leg_at = (n_heads * 2 // 16, n_heads * 10 // 16)

    @pl.loop(0, n_heads)
    def _(c):
        pl.when(c == leg_at[0])(first_leg)
        pl.when(c == leg_at[1])(second_leg)
        head(c)

    pl.loop(0, n_chunks)(before_place)

    wait_on(rsem.at[1], CS.at[pl.ds(0, n_leaf - 1)])
    codes = CS[...].reshape(n_leaf * n_graph, 128).T
    mine = codes[:cap]
    for i in range(1, half):
        mine = jnp.where(lax.rem(l, half) == i, codes[i * cap : (i + 1) * cap], mine)
    mine = jnp.concatenate([mine[: cap // 2], mine[cap // 2 :]], 1).astype(BF16)
    MACC[...] = jnp.zeros_like(MACC)

    def place(c):
        cols = pl.ds(pl.multiple_of(c * chunk, chunk), chunk)
        picked = mm(mine, OD[:, cols])
        in_row = iota((cap // 2, chunk), 0) == (sslot[:, cols] & (cap // 2 - 1))
        atom_box = jnp.sum(jnp.where(in_row, picked, 0.0), 0, keepdims=True)
        ob = one_hot(atom_box.astype(jnp.int32), box_dev)
        OB[:, cols] = ob
        MACC[...] += mm(BLK[:, cols], ob, NT)

    pl.loop(0, n_chunks)(place)

    rows = n_leaf * 8
    part = MACC[...]
    MX[8 : rows + 8, :] = part
    MX[:8, :] = part[rows - 8 :]
    MX[rows + 8 :, :] = part[:8]
    P1[l] = MX[pl.ds(pl.multiple_of(l * 8, 8), 24), :]
    to_leaf(4, lambda peer: MX.at[pl.ds(pl.multiple_of(peer * 8, 8), 24)], P1.at[l])

    sub = iota((8, 128), 0)

    def build(dst, code_row, groups):
        def step(k, masks):
            row = code_row(k) - sub
            return tuple(m + jnp.where(row == 8 * i, 1.0, 0.0) for i, m in zip(groups, masks))

        zero = tuple(jnp.zeros((8, 128), F32) for _ in groups)
        masks = lax.fori_loop(0, lbox.shape[0], step, zero, unroll=4)
        for i, m in zip(groups, masks):
            dst[8 * i : 8 * i + 8, :] = m

    last = 8 * (n_grp - 1) + 4
    outer = (n_grp // 5) * 2
    inner = range(n_grp // 5, n_grp - n_grp // 5)
    build(F, lambda k: LCODE[pl.ds(k, 1), :], range(n_grp))
    build(G, lambda k: last - LCODE[pl.ds(k, 1), :], inner)
    wait_on(rsem.at[2], LN.at[0])
    wait_on(rsem.at[3], LN.at[1])
    build(GN.at[0], lambda k: last - LN[0, pl.ds(k, 1), :], range(outer))
    build(GN.at[1], lambda k: last - LN[1, pl.ds(k, 1), :], range(n_grp - outer, n_grp))
    for i in range(n_grp):
        at = pl.ds(8 * i, 8)
        slabs = [
            shift_x(ref[at, :]) if i in used else None
            for ref, used in (
                (GN.at[0], range(outer)), (G, inner), (GN.at[1], range(n_grp - outer, n_grp)),
            )
        ]
        R[at, :] = shift_y(shift_z(slabs, i // 5 - 2), i % 5 - 2)
    ACC[...] = jnp.zeros_like(ACC)
    OGACC[...] = jnp.zeros_like(OGACC)
    IBACC[...] = jnp.zeros_like(IBACC)
    cut = [n_chunks * i // 4 for i in range(5)]
    pl.loop(cut[0], cut[1])(before_grad)

    wait_on(rsem.at[4], P1.at[pl.ds(0, n_leaf - 1)])
    total = jnp.sum(P1[...], 0)

    total = roll(total, -2)
    lower = iota((8, 128), 1) < 64
    shifted = []
    for ch in range(8):
        planes = []
        for s in range(3):
            row = total[8 * s + ch : 8 * s + ch + 1]
            slab = wrap_x(pltpu.roll(jnp.broadcast_to(row, (8, 128)), 0, 1, stride=1, stride_axis=0))
            swapped = roll(slab, 64)
            planes += [jnp.where(lower, slab, swapped), jnp.where(lower, swapped, slab)]
        shifted.append([[roll(x, -8 * dy) if dy else x for dy in range(-2, 3)] for x in planes])
    off_x = (2 - iota((8, 128), 0)).astype(F32)
    sums = [jnp.zeros((8, 128), F32) for _ in range(8)]
    for i in range(n_grp):
        off_z, off_y = i // 5 - 2, i % 5 - 2
        dist = jnp.maximum(off_x * off_x + float(off_z * off_z + off_y * off_y), 1.0)
        inv = lax.rsqrt(dist)
        cube = inv * inv * inv
        three = 3.0 * inv * inv
        for base, mask in ((0, F), (4, R)):
            m = mask[8 * i : 8 * i + 8, :]
            q0, q1, q2, q3 = [
                m * jnp.where(lower, *(shifted[base + j][off_z + p][off_y + 2] for p in (2, 3)))
                for j in range(4)
            ]
            proj = off_x * q1 + float(off_y) * q2 + float(off_z) * q3
            sums[base] += q0 * inv - proj * cube
            radial = q0 - three * proj
            sums[base + 1] += (radial * off_x + q1) * cube
            sums[base + 2] += (radial * float(off_y) + q2) * cube
            sums[base + 3] += (radial * float(off_z) + q3) * cube
    for j in range(8):
        TO[j : j + 1, :] = jnp.sum(sums[j], 0, keepdims=True)
    to_core(5, TO, TX)
    wait_on(rsem.at[5], TX)
    TC[...] = TO[...] + TX[...]
    TB[zpos * n_leaf + l] = TC[...]
    to_chips(6, TC, TB.at[zpos * n_leaf + l])
    pl.loop(cut[1], cut[4])(before_grad)
    wait_on(rsem.at[6], TB.at[pl.ds(0, n_z * n_leaf - 1)])
    table = jnp.sum(TB[...].reshape(n_z, rows, 128), 0)
    hi = table.astype(BF16)
    table = jnp.concatenate([hi, (table - hi.astype(F32)).astype(BF16)], 1)

    def backward(c):
        cols = pl.ds(pl.multiple_of(c * chunk, chunk), chunk)
        src_leaf = (sslot[:, cols] >> cap_bits) & (n_leaf - 1)
        ob = OB[:, cols]
        got = mm(table, jnp.concatenate([ob, ob], 0))
        field = jnp.zeros((8, chunk), F32)
        for i in range(n_leaf):
            field += jnp.where(src_leaf == i, got[8 * i : 8 * i + 8], 0.0)
        FIELD[:, cols] = field
        sub = iota((8, chunk), 0)
        terms = field * U[:, cols] * jnp.where(sub < 4, scale_row(cols), 1.0)
        grad = jnp.sum(terms, 0, keepdims=True)
        grad = jnp.broadcast_to(grad, (16, chunk)).astype(BF16)
        GR[:, cols] = grad
        grad = grad[None]

        def scaled(ref):
            x = ref[:, cols].reshape(hid // 16, 16, chunk) * grad
            return x.reshape(hid, chunk)

        ACC[0] += mm(A1[:, cols], scaled(SL2), NT)
        slope = scaled(SL1)
        SL1[:, cols] = slope
        ACC[1, :hid, :] += mm(slope, X[cols, :])

    pl.loop(0, n_chunks)(backward)

    BOTH[...] = ACC[:, :hid, :].astype(BF16)
    to_core(7, BOTH.at[1 - core], RX)

    def to_row(columns):
        return jnp.sum(columns.T, 0, keepdims=True)

    wait_on(rsem.at[7], RX)
    SB[...] = (ACC[core, :hid, :] + RX[...].astype(F32)).astype(BF16)
    RM[l] = SB[pl.ds(pl.multiple_of(l * wrow, wrow), wrow), :]
    to_leaf(9, lambda peer: SB.at[pl.ds(pl.multiple_of(peer * wrow, wrow), wrow)], RM.at[l])
    def out_copy(c):
        rows = pl.ds(c * chunk, chunk)
        return pltpu.make_async_copy(X.at[rows], fgrad.at[rows], osem.at[c])

    def backward_row(c):
        at = pl.ds(pl.multiple_of(c * chunk, chunk), chunk)
        X[at, :] = mm(SL1[:, at], W1T[...], TN).astype(BF16)
        out_copy(c).start()
        IBACC[...] += fold_lanes(SL1[:, at].astype(F32))
        og = A2[:, at].reshape(hid // 16, 16, chunk) * GR[:, at][None]
        OGACC[...] += fold_lanes(og.reshape(hid, chunk).astype(F32))
        q = Q[:, at]
        force = FIELD[:, at] * jnp.where(iota((8, chunk), 0) < 4, scale_row(at) * q, q)
        force = force + pltpu.roll(force, 4, 0)
        PG[:, at] = force[1:4]

    pl.loop(0, n_chunks)(backward_row)
    force_copy = pltpu.make_async_copy(PG, pgrad, isem.at[0])
    force_copy.start()
    BV[...] = jnp.zeros_like(BV)
    vectors = (ACC[0, hid : hid + 1, :], to_row(OGACC[...]), to_row(IBACC[...]))
    for i, vector in enumerate(vectors):
        for j in range(hid // 128):
            at = 2 * i + j
            BV[at : at + 1, :] = vector[:, 128 * j : 128 * j + 128]
    BX[core] = BV[...]
    to_core(8, BV, BX.at[core])
    wait_on(rsem.at[8], BV)
    BC[...] = BX[0] + BX[1]
    BL[l] = BC[...]
    to_leaf(10, lambda peer: BC, BL.at[l])

    wait_on(rsem.at[9], RM.at[pl.ds(0, n_leaf - 1)])
    GS[...] = jnp.sum(RM[...].astype(F32), 0).astype(BF16)
    GM[zpos] = GS[...]
    to_z(11, GS, GM.at[zpos])
    wait_on(rsem.at[11], GM.at[pl.ds(0, n_z - 1)])
    AS[...] = jnp.sum(GM[...].astype(F32), 0).astype(BF16)
    AM[l] = AS[...]
    to_leaf(13, lambda peer: AS, AM.at[l])
    wait_on(rsem.at[10], BL.at[pl.ds(0, n_leaf - 1)])
    BS[...] = jnp.sum(BL[...], 0)
    BG[zpos] = BS[...]
    to_z(12, BS, BG.at[zpos])
    wait_on(rsem.at[12], BG.at[pl.ds(0, n_z - 1)])
    BF[...] = jnp.sum(BG[...], 0)
    bias_copy = pltpu.make_async_copy(BF, bias_out, isem.at[1])
    bias_copy.start()
    wait_on(rsem.at[13], AM.at[pl.ds(0, n_leaf - 1)])
    to_core(14, AM, AO)
    mine_copy = pltpu.make_async_copy(AM, mats.at[core], isem.at[2])
    mine_copy.start()

    leaf_sent = pl.ds(0, n_leaf - 1)
    graph_sent = pl.ds(0, n_graph - 1)
    z_sent = pl.ds(0, n_z - 1)
    sent = {
        0: CA.at[graph_sent], 1: CS.at[leaf_sent], 2: LN.at[0], 3: LN.at[1], 4: P1.at[leaf_sent],
        5: TX, 6: TB.at[pl.ds(0, n_z * n_leaf - 1)], 7: RX, 8: BV, 9: RM.at[leaf_sent],
        10: BL.at[leaf_sent], 11: GM.at[z_sent], 12: BG.at[z_sent], 13: AM.at[leaf_sent], 14: AO,
    }
    for k, view in sent.items():
        wait_on(ssem.at[k], view)

    @pl.loop(0, n_chunks)
    def _(c):
        out_copy(c).wait()

    force_copy.wait()
    bias_copy.wait()
    wait_on(rsem.at[14], AO)
    other_copy = pltpu.make_async_copy(AO, mats.at[1 - core], isem.at[3])
    other_copy.start()
    mine_copy.wait()
    other_copy.wait()


def finish(
    pieces, fgrad, pgrad, mats, bias, fout, pout, ing, inb, midg, midb, outg,
    FH, PH, MH, BH, IN, MID, IB, MB, OG, lsem, ssem,
):
    rows = FH.shape[0] // pieces
    legs = [
        (fgrad.at[pl.ds(i * rows, rows)], FH.at[pl.ds(i * rows, rows)], fout.at[pl.ds(i * rows, rows)])
        for i in range(pieces)
    ]
    legs.append((pgrad, PH, pout))
    loads = [pltpu.make_async_copy(a, b, lsem.at[i]) for i, (a, b, _) in enumerate(legs)]
    stores = [pltpu.make_async_copy(b, c, ssem.at[i]) for i, (_, b, c) in enumerate(legs)]
    last = len(legs)
    loads.append(pltpu.make_async_copy(mats, MH, lsem.at[last]))
    loads.append(pltpu.make_async_copy(bias, BH, lsem.at[last + 1]))
    for load in loads:
        load.start()
    for load, store in zip(loads, stores):
        load.wait()
        store.start()
    for load in loads[last:]:
        load.wait()
    hid = MID.shape[0]
    MID[...] = MH[0].astype(F32).reshape(hid, hid)
    IN[...] = MH[1].astype(F32).reshape(hid, hid).T
    for i, row in enumerate((MB, OG, IB)):
        for j in range(hid // 128):
            row[:, 128 * j : 128 * j + 128] = BH[2 * i + j : 2 * i + j + 1, :]
    for i, (a, b) in enumerate(((IN, ing), (MID, midg), (IB, inb), (MB, midb), (OG, outg))):
        stores.append(pltpu.make_async_copy(a, b, ssem.at[last + i]))
        stores[-1].start()
    for store in stores:
        store.wait()


def body(
    features, positions, energy_weight, send_slot, tile_slot, box_count, list_box, list_image,
    w_in, b_in, w_mid, b_mid, w_out,
):
    n_graph, n_leaf = lax.axis_size("graph"), lax.axis_size("leaf")
    atoms, feat = features.shape
    hid = w_in.shape[1]
    head_chunk = min(HEAD_CHUNK, atoms // 4)
    chunk = min(CHUNK, atoms // 2)
    n_grp = 25
    n_z = n_graph // 2
    code_rows = n_leaf * (atoms // (n_graph * n_leaf)) // 128
    wrow = hid // n_leaf
    any_space = pl.BlockSpec(memory_space=pl.ANY)

    def v(shape, dtype=F32):
        return pltpu.VMEM(shape, dtype)

    scratch = [
        v((atoms, feat), BF16), v((hid + 16, atoms), BF16), v((hid, atoms), BF16),
        v((hid, atoms), BF16), v((hid, atoms), BF16), v((128, atoms), BF16),
        v((2 * n_leaf * n_graph, atoms), BF16), v((n_leaf * 8, atoms), BF16),
        v((8, atoms)), v((1, atoms)),
        v((hid, feat), BF16), v((hid, feat), BF16), v((hid, hid), BF16), v((hid, hid), BF16),
        v((hid, 128)), v((hid, 128)), v((hid, 128)), v((hid, 128)),
        v((atoms // 128, 128)), v((n_graph, code_rows, 128)), v((code_rows, n_graph, 128)),
        v((n_leaf, n_graph, 128)),
        v((8 * n_grp, 128)), v((8 * n_grp, 128)), v((2, 8 * n_grp, 128)), v((8 * n_grp, 128)),
        v((list_box.shape[1], 128), jnp.int32), v((2, list_box.shape[1], 128), jnp.int32),
        v((n_leaf * 8, 128)),
        v((n_leaf * 8 + 16, 128)), v((n_leaf, 24, 128)),
        v((8, 128)), v((8, 128)), v((8, 128)), v((n_z * n_leaf, 8, 128)),
        v((2, hid + 16, hid)), v((hid, 128)), v((hid, 128)),
        v((2, hid, hid), BF16), v((hid, hid), BF16), v((hid, hid), BF16),
        v((n_leaf, wrow, hid), BF16), v((wrow, hid), BF16), v((n_z, wrow, hid), BF16),
        v((wrow, hid), BF16), v((n_leaf, wrow, hid), BF16), v((n_leaf, wrow, hid), BF16),
        v((8, 128)), v((2, 8, 128)), v((8, 128)), v((n_leaf, 8, 128)), v((8, 128)),
        v((n_z, 8, 128)), v((8, 128)), v((16, atoms), BF16), v((8, atoms)), v((3, atoms)),
        pltpu.SemaphoreType.DMA((atoms // head_chunk,)), pltpu.SemaphoreType.DMA((atoms // chunk,)),
        pltpu.SemaphoreType.DMA((12,)), pltpu.SemaphoreType.DMA((15,)),
        pltpu.SemaphoreType.DMA((15,)),
    ]
    sds = jax.ShapeDtypeStruct
    shapes = (
        sds((atoms, feat), BF16), sds((3, atoms), F32),
        sds((feat, hid), F32), sds((1, hid), F32),
        sds((hid, hid), F32), sds((1, hid), F32), sds((1, hid), F32),
    )
    mids = (
        shapes[0], shapes[1], sds((2, n_leaf, wrow, hid), BF16), sds((8, 128), F32),
    )
    ins = (
        positions, energy_weight.reshape(1, atoms), send_slot.reshape(1, atoms),
        tile_slot.reshape(atoms // 128, 128), box_count.reshape(1, -1), list_box.T,
        list_image.transpose(0, 2, 1), w_in, b_in.reshape(1, hid), w_mid, b_mid.reshape(1, hid),
        w_out.reshape(hid // 128, 128),
    )
    held = [
        (pltpu.SMEM if i == 4 else pltpu.VMEM)(x.shape, x.dtype) for i, x in enumerate(ins)
    ]
    mids = pl.pallas_call(
        functools.partial(kernel, n_graph, n_leaf, head_chunk, chunk, n_grp),
        out_shape=mids,
        in_specs=[any_space] * 13,
        out_specs=(any_space,) * 4,
        scratch_shapes=held + scratch,
        compiler_params=pltpu.CompilerParams(
            collective_id=0, has_side_effects=True, vmem_limit_bytes=56 * 1024 * 1024
        ),
        name="latent_charge",
    )(features, *ins)
    pieces = 4
    outs = pl.pallas_call(
        functools.partial(finish, pieces),
        out_shape=shapes,
        in_specs=[any_space] * 4,
        out_specs=(any_space,) * len(shapes),
        scratch_shapes=[v(x.shape, x.dtype) for x in mids]
        + [v(shapes[i].shape) for i in (2, 4, 3, 5, 6)]
        + [pltpu.SemaphoreType.DMA((pieces + 3,)), pltpu.SemaphoreType.DMA((pieces + 6,))],
        compiler_params=pltpu.CompilerParams(vmem_limit_bytes=56 * 1024 * 1024),
        name="results",
    )(*mids)
    fgrad, pgrad, ing, inb, midg, midb, outg = outs
    return (fgrad, pgrad, ing, inb.reshape(hid), midg, midb.reshape(hid), outg.reshape(hid))


def solution(mesh):
    placed = (
        P(("graph", "leaf"), None),
        P(None, ("graph", "leaf")),
        P(("graph", "leaf")),
        P(("graph", "leaf")),
        P(("graph", "leaf")),
        P("leaf", "graph"),
        P("leaf", None),
        P(None, "leaf", None),
        P(), P(), P(), P(), P(),
    )
    return jax.shard_map(
        body,
        mesh=mesh,
        in_specs=placed,
        out_specs=(P(("graph", "leaf"), None), P(None, ("graph", "leaf")), P(), P(), P(), P(), P()),
        check_vma=False,
    )
```

```python
import functools

import jax
import jax.numpy as jnp
from jax import lax
from jax.experimental import pallas as pl
from jax.experimental.pallas import tpu as pltpu
from jax.sharding import PartitionSpec as P

MESH = pl.DeviceIdType.MESH
F32 = jnp.float32
BF16 = jnp.bfloat16
COUPLING = 0.5
SLOT_DEV = 128
HEAD_CHUNK = 1024
CHUNK = 4096
NT = (((1,), (1,)), ((), ()))
NN = (((1,), (0,)), ((), ()))
TN = (((0,), (0,)), ((), ()))


def mm(a, b, dims=NN):
    return lax.dot_general(a, b, dims, preferred_element_type=F32)


def iota(shape, axis):
    return lax.broadcasted_iota(jnp.int32, shape, axis)


def tile_lanes(x, n):
    return jnp.concatenate([x] * (n // x.shape[1]), 1)


def fold_lanes(x):
    parts = [x[:, i : i + 128] for i in range(0, x.shape[1], 128)]
    total = parts[0]
    for part in parts[1:]:
        total = total + part
    return total


def roll(x, shift):
    return pltpu.roll(x, shift % 128, 1)


def shift_x(x):
    return wrap_x(roll(pltpu.roll(x, 120, 1, stride=1, stride_axis=0), 6))


def wrap_x(first):
    x = first
    col = iota(x.shape, 1) % 8 + 2 - iota(x.shape, 0)
    return jnp.where(col > 7, roll(first, 8), jnp.where(col < 0, roll(first, -8), first))


def shift_y(x, dy):
    if dy == 0:
        return x
    straight = roll(x, -8 * dy)
    row = (iota(x.shape, 1) // 8) % 8 + dy
    return jnp.where((row >= 0) & (row < 8), straight, roll(straight, 64))


def shift_z(slabs, dz):
    if dz % 2 == 0:
        return slabs[dz // 2 + 1]
    low, high = (0, 1) if dz == -1 else (1, 2)
    lower = iota(slabs[low].shape, 1) < 64
    return jnp.where(lower, roll(slabs[low], 64), roll(slabs[high], 64))


def kernel(
    n_graph, n_leaf, head_chunk, chunk, n_grp,
    feat, *refs,
):
    ins, refs = refs[:12], refs[12:]
    outs, refs = refs[:4], refs[4:]
    (pos, ew, sslot, tslot, count, lbox, limg, w_in, b_in, w_mid, b_mid, w_out), refs = (
        refs[:12], refs[12:],
    )
    fgrad, pgrad, mats, bias_out = outs
    (
    X, A1, SL1, A2, SL2, OB, OD, BLK, U, Q, W1H, W1T, W2TH, W2H, B1, B2, WO, WOH,
    CODE, CA, CB, CS, F, G, GN, R, LCODE, LN, MACC, MX, P1, TO, TX, TC, TB,
    ACC, OGACC, IBACC, BOTH, RX, SB, RM, GS, GM, AS, AM,
    BV, BX, BC, BL, BS, BG, BF, GR, FIELD, PG,
    xsem, osem, isem, ssem, rsem,
    ) = refs
    g = lax.axis_index("graph")
    l = lax.axis_index("leaf")
    core = lax.rem(g, 2)
    zpos = g // 2
    atoms = X.shape[0]
    hid = SL1.shape[0]
    cap = atoms // (n_graph * n_leaf)
    leaf_bits = n_leaf.bit_length() - 1
    cap_bits = cap.bit_length() - 1
    code_rows = n_leaf * cap // 128
    box_dev = 128
    wrow = hid // n_leaf
    n_z = n_graph // 2
    n_heads = atoms // head_chunk
    n_chunks = atoms // chunk

    def leaf_peer(o):
        return lax.rem(l + o, n_leaf)

    def send(k, src, dst, device):
        pltpu.make_async_remote_copy(
            src_ref=src, dst_ref=dst, send_sem=ssem.at[k], recv_sem=rsem.at[k],
            device_id=device, device_id_type=MESH,
        ).start()

    def to_leaf(k, src_of, dst):
        @pl.loop(1, n_leaf, unroll=3)
        def _(o):
            peer = leaf_peer(o)
            send(k, src_of(peer), dst, (g, peer))

    def to_graph(k, src_of, dst):
        @pl.loop(1, n_graph)
        def _(o):
            peer = lax.rem(g + o, n_graph)
            send(k, src_of(peer), dst, (peer, l))

    def to_z(k, src, dst):
        @pl.loop(1, n_z)
        def _(o):
            send(k, src, dst, (lax.rem(g + 2 * o, n_graph), l))

    def to_chips(k, src, dst):
        mine = zpos * n_leaf + l

        @pl.loop(1, n_z * n_leaf, unroll=7 if n_z * n_leaf == 64 else 1)
        def _(o):
            chip = lax.rem(mine + o, n_z * n_leaf)
            send(k, src, dst, (2 * (chip // n_leaf) + core, lax.rem(chip, n_leaf)))

    def to_core(k, src, dst):
        send(k, src, dst, (g + 1 - 2 * core, l))

    def wait_on(sem, view):
        pltpu.make_async_copy(view, view, sem).wait()

    bar = pltpu.get_barrier_semaphore()

    @pl.loop(1, n_leaf)
    def _(o):
        pl.semaphore_signal(bar, inc=1, device_id=(g, leaf_peer(o)), device_id_type=MESH)

    @pl.loop(1, n_graph)
    def _(o):
        pl.semaphore_signal(
            bar, inc=1, device_id=(lax.rem(g + o, n_graph), l), device_id_type=MESH
        )

    def feat_copy(c):
        rows = pl.ds(c * head_chunk, head_chunk)
        return pltpu.make_async_copy(feat.at[rows], X.at[rows], xsem.at[c])

    fetches = [
        pltpu.make_async_copy(src, dst, isem.at[i])
        for i, (src, dst) in enumerate(
            zip(ins, (pos, ew, sslot, tslot, count, lbox, limg, w_in, b_in, w_mid, b_mid, w_out))
        )
    ]
    for fetch in fetches:
        fetch.start()

    @pl.loop(0, n_heads)
    def _(c):
        feat_copy(c).start()

    for fetch in fetches:
        fetch.wait()

    slot = tslot[...]
    box = slot >> 7

    def count_step(b, cnt):
        return jnp.where(box == b, count[0, b], cnt)

    cnt = lax.fori_loop(0, box_dev, count_step, jnp.zeros_like(slot), unroll=8)
    CODE[...] = jnp.where((slot & (SLOT_DEV - 1)) < cnt, box, -1).astype(F32)
    CA[g] = CODE[pl.ds(pl.multiple_of(g * code_rows, code_rows), code_rows), :]

    w1 = w_in[...].astype(F32).T
    W1T[...] = w1.astype(BF16)
    W1H[...] = (0.5 * w1).astype(BF16)
    w2 = w_mid[...].astype(F32)
    W2H[...] = (0.5 * w2).astype(BF16)
    W2TH[...] = (0.5 * w2.T).astype(BF16)

    def column(row):
        return jnp.broadcast_to(row, (128, row.shape[1])).T

    B1[...] = column(0.5 * b_in[...])
    B2[...] = column(0.5 * b_mid[...])
    for i in range(hid // 128):
        wo = column(w_out[i : i + 1, :].astype(F32))
        WO[128 * i : 128 * i + 128, :] = wo
        WOH[128 * i : 128 * i + 128, :] = 0.5 * wo
    A1[hid:, :] = jnp.ones((A1.shape[0] - hid, atoms), BF16)
    U[...] = jnp.ones_like(U)
    U[1:4, :] = pos[...]
    U[5:8, :] = pos[...]

    own = l * box_dev + iota((lbox.shape[0], box_dev), 1)
    src = lbox[...]
    dims = (8, 8, n_leaf * box_dev // 64)
    dx, dy, dz = [
        coord(src) + limg[i] * dims[i] - coord(own)
        for i, coord in enumerate([lambda b: b & 7, lambda b: (b >> 3) & 7, lambda b: b >> 6])
    ]
    LCODE[...] = ((dz + 2) * 5 + dy + 2) * 8 + 2 - dx

    def scale_row(cols):
        return (0.5 * COUPLING) * ew[:, cols]

    def one_hot(index, n):
        hit = iota((n, chunk), 0).astype(BF16) == index.astype(BF16)
        return jnp.where(hit, BF16(1), BF16(0))

    def head(c):
        feat_copy(c).wait()
        at = pl.ds(pl.multiple_of(c * head_chunk, head_chunk), head_chunk)
        h = mm(W1H[...], X[at, :], NT) + tile_lanes(B1[...], head_chunk)
        t = jnp.tanh(h)
        a = (h + h * t).astype(BF16)
        t = t.astype(BF16)
        A1[:hid, at] = a
        SL1[:, at] = (1 + a) + t * (1 - a)
        h = mm(W2TH[...], a) + tile_lanes(B2[...], head_chunk)
        t = jnp.tanh(h)
        wo = tile_lanes(WO[...], head_chunk)
        a = h + h * t
        Q[:, at] = jnp.sum(a * wo, 0, keepdims=True)
        A2[:, at] = a.astype(BF16)
        half_wo = tile_lanes(WOH[...], head_chunk)
        SL2[:, at] = (((1.0 + a) + t * (1.0 - a)) * half_wo).astype(BF16)

    def before_place(c):
        cols = pl.ds(pl.multiple_of(c * chunk, chunk), chunk)
        s = sslot[:, cols]
        src_leaf = (s >> cap_bits) & (n_leaf - 1)
        row = src_leaf * n_graph + (s >> (cap_bits + leaf_bits))
        row = row + ((s >> (cap_bits - 1)) & 1) * (n_leaf * n_graph)
        OD[:, cols] = one_hot(row, 2 * n_leaf * n_graph)
        q = Q[:, cols]
        sub = iota((8, chunk), 0)
        vals = U[:, cols] * jnp.where(sub < 4, q, scale_row(cols) * q)
        blocks = [jnp.where(src_leaf == i, vals, 0.0) for i in range(n_leaf)]
        BLK[:, cols] = jnp.concatenate(blocks, 0).astype(BF16)

    def before_grad(c):
        cols = pl.ds(pl.multiple_of(c * chunk, chunk), chunk)
        slope = mm(W2H[...], SL2[:, cols]) * SL1[:, cols].astype(F32)
        SL1[:, cols] = slope.astype(BF16)

    def first_leg():
        pl.semaphore_wait(bar, n_leaf + n_graph - 2)
        to_graph(
            0,
            lambda peer: CODE.at[pl.ds(pl.multiple_of(peer * code_rows, code_rows), code_rows)],
            CA.at[g],
        )
        send(2, LCODE, LN.at[0], (g, leaf_peer(1)))
        send(3, LCODE, LN.at[1], (g, leaf_peer(n_leaf - 1)))

    half = 128 // cap

    def second_leg():
        wait_on(rsem.at[0], CA.at[pl.ds(0, n_graph - 1)])
        flat = CA[...]
        for r in range(code_rows):
            CB[r] = flat[:, r, :]
        CS[l] = CB[l // half]
        to_leaf(1, lambda peer: CB.at[peer // half], CS.at[l])

    leg_at = (n_heads * 2 // 16, n_heads * 10 // 16)

    @pl.loop(0, n_heads)
    def _(c):
        pl.when(c == leg_at[0])(first_leg)
        pl.when(c == leg_at[1])(second_leg)
        head(c)

    pl.loop(0, n_chunks)(before_place)

    wait_on(rsem.at[1], CS.at[pl.ds(0, n_leaf - 1)])
    codes = CS[...].reshape(n_leaf * n_graph, 128).T
    mine = codes[:cap]
    for i in range(1, half):
        mine = jnp.where(lax.rem(l, half) == i, codes[i * cap : (i + 1) * cap], mine)
    mine = jnp.concatenate([mine[: cap // 2], mine[cap // 2 :]], 1).astype(BF16)
    MACC[...] = jnp.zeros_like(MACC)

    def place(c):
        cols = pl.ds(pl.multiple_of(c * chunk, chunk), chunk)
        picked = mm(mine, OD[:, cols])
        in_row = iota((cap // 2, chunk), 0) == (sslot[:, cols] & (cap // 2 - 1))
        atom_box = jnp.sum(jnp.where(in_row, picked, 0.0), 0, keepdims=True)
        ob = one_hot(atom_box.astype(jnp.int32), box_dev)
        OB[:, cols] = ob
        MACC[...] += mm(BLK[:, cols], ob, NT)

    pl.loop(0, n_chunks)(place)

    rows = n_leaf * 8
    part = MACC[...]
    MX[8 : rows + 8, :] = part
    MX[:8, :] = part[rows - 8 :]
    MX[rows + 8 :, :] = part[:8]
    P1[l] = MX[pl.ds(pl.multiple_of(l * 8, 8), 24), :]
    to_leaf(4, lambda peer: MX.at[pl.ds(pl.multiple_of(peer * 8, 8), 24)], P1.at[l])

    sub = iota((8, 128), 0)

    def build(dst, code_row, groups):
        def step(k, masks):
            row = code_row(k) - sub
            return tuple(m + jnp.where(row == 8 * i, 1.0, 0.0) for i, m in zip(groups, masks))

        zero = tuple(jnp.zeros((8, 128), F32) for _ in groups)
        masks = lax.fori_loop(0, lbox.shape[0], step, zero, unroll=4)
        for i, m in zip(groups, masks):
            dst[8 * i : 8 * i + 8, :] = m

    last = 8 * (n_grp - 1) + 4
    outer = (n_grp // 5) * 2
    inner = range(n_grp // 5, n_grp - n_grp // 5)
    build(F, lambda k: LCODE[pl.ds(k, 1), :], range(n_grp))
    build(G, lambda k: last - LCODE[pl.ds(k, 1), :], inner)
    wait_on(rsem.at[2], LN.at[0])
    wait_on(rsem.at[3], LN.at[1])
    build(GN.at[0], lambda k: last - LN[0, pl.ds(k, 1), :], range(outer))
    build(GN.at[1], lambda k: last - LN[1, pl.ds(k, 1), :], range(n_grp - outer, n_grp))
    for i in range(n_grp):
        at = pl.ds(8 * i, 8)
        slabs = [
            shift_x(ref[at, :]) if i in used else None
            for ref, used in (
                (GN.at[0], range(outer)), (G, inner), (GN.at[1], range(n_grp - outer, n_grp)),
            )
        ]
        R[at, :] = shift_y(shift_z(slabs, i // 5 - 2), i % 5 - 2)
    ACC[...] = jnp.zeros_like(ACC)
    OGACC[...] = jnp.zeros_like(OGACC)
    IBACC[...] = jnp.zeros_like(IBACC)
    cut = [n_chunks * i // 4 for i in range(5)]
    pl.loop(cut[0], cut[1])(before_grad)

    wait_on(rsem.at[4], P1.at[pl.ds(0, n_leaf - 1)])
    total = jnp.sum(P1[...], 0)

    total = roll(total, -2)
    lower = iota((8, 128), 1) < 64
    shifted = []
    for ch in range(8):
        planes = []
        for s in range(3):
            row = total[8 * s + ch : 8 * s + ch + 1]
            slab = wrap_x(pltpu.roll(jnp.broadcast_to(row, (8, 128)), 0, 1, stride=1, stride_axis=0))
            swapped = roll(slab, 64)
            planes += [jnp.where(lower, slab, swapped), jnp.where(lower, swapped, slab)]
        shifted.append([[roll(x, -8 * dy) if dy else x for dy in range(-2, 3)] for x in planes])
    off_x = (2 - iota((8, 128), 0)).astype(F32)
    sums = [jnp.zeros((8, 128), F32) for _ in range(8)]
    for i in range(n_grp):
        off_z, off_y = i // 5 - 2, i % 5 - 2
        dist = jnp.maximum(off_x * off_x + float(off_z * off_z + off_y * off_y), 1.0)
        inv = lax.rsqrt(dist)
        cube = inv * inv * inv
        three = 3.0 * inv * inv
        for base, mask in ((0, F), (4, R)):
            m = mask[8 * i : 8 * i + 8, :]
            q0, q1, q2, q3 = [
                m * jnp.where(lower, *(shifted[base + j][off_z + p][off_y + 2] for p in (2, 3)))
                for j in range(4)
            ]
            proj = off_x * q1 + float(off_y) * q2 + float(off_z) * q3
            sums[base] += q0 * inv - proj * cube
            radial = q0 - three * proj
            sums[base + 1] += (radial * off_x + q1) * cube
            sums[base + 2] += (radial * float(off_y) + q2) * cube
            sums[base + 3] += (radial * float(off_z) + q3) * cube
    for j in range(8):
        TO[j : j + 1, :] = jnp.sum(sums[j], 0, keepdims=True)
    to_core(5, TO, TX)
    wait_on(rsem.at[5], TX)
    TC[...] = TO[...] + TX[...]
    TB[zpos * n_leaf + l] = TC[...]
    to_chips(6, TC, TB.at[zpos * n_leaf + l])
    pl.loop(cut[1], cut[4])(before_grad)
    wait_on(rsem.at[6], TB.at[pl.ds(0, n_z * n_leaf - 1)])
    table = jnp.sum(TB[...].reshape(n_z, rows, 128), 0)
    hi = table.astype(BF16)
    table = jnp.concatenate([hi, (table - hi.astype(F32)).astype(BF16)], 1)

    def backward(c):
        cols = pl.ds(pl.multiple_of(c * chunk, chunk), chunk)
        src_leaf = (sslot[:, cols] >> cap_bits) & (n_leaf - 1)
        ob = OB[:, cols]
        got = mm(table, jnp.concatenate([ob, ob], 0))
        field = jnp.zeros((8, chunk), F32)
        for i in range(n_leaf):
            field += jnp.where(src_leaf == i, got[8 * i : 8 * i + 8], 0.0)
        FIELD[:, cols] = field
        sub = iota((8, chunk), 0)
        terms = field * U[:, cols] * jnp.where(sub < 4, scale_row(cols), 1.0)
        grad = jnp.sum(terms, 0, keepdims=True)
        grad = jnp.broadcast_to(grad, (16, chunk)).astype(BF16)
        GR[:, cols] = grad
        grad = grad[None]

        def scaled(ref):
            x = ref[:, cols].reshape(hid // 16, 16, chunk) * grad
            return x.reshape(hid, chunk)

        ACC[0] += mm(A1[:, cols], scaled(SL2), NT)
        slope = scaled(SL1)
        SL1[:, cols] = slope
        ACC[1, :hid, :] += mm(slope, X[cols, :])

    pl.loop(0, n_chunks)(backward)

    BOTH[...] = ACC[:, :hid, :].astype(BF16)
    to_core(7, BOTH.at[1 - core], RX)

    def to_row(columns):
        return jnp.sum(columns.T, 0, keepdims=True)

    wait_on(rsem.at[7], RX)
    SB[...] = (ACC[core, :hid, :] + RX[...].astype(F32)).astype(BF16)
    RM[l] = SB[pl.ds(pl.multiple_of(l * wrow, wrow), wrow), :]
    to_leaf(9, lambda peer: SB.at[pl.ds(pl.multiple_of(peer * wrow, wrow), wrow)], RM.at[l])
    def out_copy(c):
        rows = pl.ds(c * chunk, chunk)
        return pltpu.make_async_copy(X.at[rows], fgrad.at[rows], osem.at[c])

    def backward_row(c):
        at = pl.ds(pl.multiple_of(c * chunk, chunk), chunk)
        X[at, :] = mm(SL1[:, at], W1T[...], TN).astype(BF16)
        out_copy(c).start()
        IBACC[...] += fold_lanes(SL1[:, at].astype(F32))
        og = A2[:, at].reshape(hid // 16, 16, chunk) * GR[:, at][None]
        OGACC[...] += fold_lanes(og.reshape(hid, chunk).astype(F32))
        q = Q[:, at]
        force = FIELD[:, at] * jnp.where(iota((8, chunk), 0) < 4, scale_row(at) * q, q)
        force = force + pltpu.roll(force, 4, 0)
        PG[:, at] = force[1:4]

    pl.loop(0, n_chunks)(backward_row)
    force_copy = pltpu.make_async_copy(PG, pgrad, isem.at[0])
    force_copy.start()
    BV[...] = jnp.zeros_like(BV)
    vectors = (ACC[0, hid : hid + 1, :], to_row(OGACC[...]), to_row(IBACC[...]))
    for i, vector in enumerate(vectors):
        for j in range(hid // 128):
            at = 2 * i + j
            BV[at : at + 1, :] = vector[:, 128 * j : 128 * j + 128]
    BX[core] = BV[...]
    to_core(8, BV, BX.at[core])
    wait_on(rsem.at[8], BV)
    BC[...] = BX[0] + BX[1]
    BL[l] = BC[...]
    to_leaf(10, lambda peer: BC, BL.at[l])

    wait_on(rsem.at[9], RM.at[pl.ds(0, n_leaf - 1)])
    GS[...] = jnp.sum(RM[...].astype(F32), 0).astype(BF16)
    GM[zpos] = GS[...]
    to_z(11, GS, GM.at[zpos])
    wait_on(rsem.at[11], GM.at[pl.ds(0, n_z - 1)])
    AS[...] = jnp.sum(GM[...].astype(F32), 0).astype(BF16)
    AM[l] = AS[...]
    to_leaf(13, lambda peer: AS, AM.at[l])
    wait_on(rsem.at[10], BL.at[pl.ds(0, n_leaf - 1)])
    BS[...] = jnp.sum(BL[...], 0)
    BG[zpos] = BS[...]
    to_z(12, BS, BG.at[zpos])
    wait_on(rsem.at[12], BG.at[pl.ds(0, n_z - 1)])
    BF[...] = jnp.sum(BG[...], 0)
    bias_copy = pltpu.make_async_copy(BF, bias_out, isem.at[1])
    bias_copy.start()
    wait_on(rsem.at[13], AM.at[pl.ds(0, n_leaf - 1)])
    to_core(14, AM, mats.at[core])
    mine_copy = pltpu.make_async_copy(AM, mats.at[core], isem.at[2])
    mine_copy.start()

    leaf_sent = pl.ds(0, n_leaf - 1)
    graph_sent = pl.ds(0, n_graph - 1)
    z_sent = pl.ds(0, n_z - 1)
    sent = {
        0: CA.at[graph_sent], 1: CS.at[leaf_sent], 2: LN.at[0], 3: LN.at[1], 4: P1.at[leaf_sent],
        5: TX, 6: TB.at[pl.ds(0, n_z * n_leaf - 1)], 7: RX, 8: BV, 9: RM.at[leaf_sent],
        10: BL.at[leaf_sent], 11: GM.at[z_sent], 12: BG.at[z_sent], 13: AM.at[leaf_sent], 14: AM,
    }
    for k, view in sent.items():
        wait_on(ssem.at[k], view)

    @pl.loop(0, n_chunks)
    def _(c):
        out_copy(c).wait()

    force_copy.wait()
    bias_copy.wait()
    mine_copy.wait()
    wait_on(rsem.at[14], mats.at[1 - core])


def finish(
    pieces, fgrad, pgrad, mats, bias, fout, pout, ing, inb, midg, midb, outg,
    FH, PH, MH, BH, IN, MID, IB, MB, OG, lsem, ssem,
):
    rows = FH.shape[0] // pieces
    legs = [
        (fgrad.at[pl.ds(i * rows, rows)], FH.at[pl.ds(i * rows, rows)], fout.at[pl.ds(i * rows, rows)])
        for i in range(pieces)
    ]
    legs.append((pgrad, PH, pout))
    loads = [pltpu.make_async_copy(a, b, lsem.at[i]) for i, (a, b, _) in enumerate(legs)]
    stores = [pltpu.make_async_copy(b, c, ssem.at[i]) for i, (_, b, c) in enumerate(legs)]
    last = len(legs)
    loads.append(pltpu.make_async_copy(mats, MH, lsem.at[last]))
    loads.append(pltpu.make_async_copy(bias, BH, lsem.at[last + 1]))
    for load in loads:
        load.start()
    for load, store in zip(loads, stores):
        load.wait()
        store.start()
    for load in loads[last:]:
        load.wait()
    hid = MID.shape[0]
    MID[...] = MH[0].astype(F32).reshape(hid, hid)
    IN[...] = MH[1].astype(F32).reshape(hid, hid).T
    for i, row in enumerate((MB, OG, IB)):
        for j in range(hid // 128):
            row[:, 128 * j : 128 * j + 128] = BH[2 * i + j : 2 * i + j + 1, :]
    for i, (a, b) in enumerate(((IN, ing), (MID, midg), (IB, inb), (MB, midb), (OG, outg))):
        stores.append(pltpu.make_async_copy(a, b, ssem.at[last + i]))
        stores[-1].start()
    for store in stores:
        store.wait()


def body(
    features, positions, energy_weight, send_slot, tile_slot, box_count, list_box, list_image,
    w_in, b_in, w_mid, b_mid, w_out,
):
    n_graph, n_leaf = lax.axis_size("graph"), lax.axis_size("leaf")
    atoms, feat = features.shape
    hid = w_in.shape[1]
    head_chunk = min(HEAD_CHUNK, atoms // 4)
    chunk = min(CHUNK, atoms // 2)
    n_grp = 25
    n_z = n_graph // 2
    code_rows = n_leaf * (atoms // (n_graph * n_leaf)) // 128
    wrow = hid // n_leaf
    any_space = pl.BlockSpec(memory_space=pl.ANY)

    def v(shape, dtype=F32):
        return pltpu.VMEM(shape, dtype)

    scratch = [
        v((atoms, feat), BF16), v((hid + 16, atoms), BF16), v((hid, atoms), BF16),
        v((hid, atoms), BF16), v((hid, atoms), BF16), v((128, atoms), BF16),
        v((2 * n_leaf * n_graph, atoms), BF16), v((n_leaf * 8, atoms), BF16),
        v((8, atoms)), v((1, atoms)),
        v((hid, feat), BF16), v((hid, feat), BF16), v((hid, hid), BF16), v((hid, hid), BF16),
        v((hid, 128)), v((hid, 128)), v((hid, 128)), v((hid, 128)),
        v((atoms // 128, 128)), v((n_graph, code_rows, 128)), v((code_rows, n_graph, 128)),
        v((n_leaf, n_graph, 128)),
        v((8 * n_grp, 128)), v((8 * n_grp, 128)), v((2, 8 * n_grp, 128)), v((8 * n_grp, 128)),
        v((list_box.shape[1], 128), jnp.int32), v((2, list_box.shape[1], 128), jnp.int32),
        v((n_leaf * 8, 128)),
        v((n_leaf * 8 + 16, 128)), v((n_leaf, 24, 128)),
        v((8, 128)), v((8, 128)), v((8, 128)), v((n_z * n_leaf, 8, 128)),
        v((2, hid + 16, hid)), v((hid, 128)), v((hid, 128)),
        v((2, hid, hid), BF16), v((hid, hid), BF16), v((hid, hid), BF16),
        v((n_leaf, wrow, hid), BF16), v((wrow, hid), BF16), v((n_z, wrow, hid), BF16),
        v((wrow, hid), BF16), v((n_leaf, wrow, hid), BF16),
        v((8, 128)), v((2, 8, 128)), v((8, 128)), v((n_leaf, 8, 128)), v((8, 128)),
        v((n_z, 8, 128)), v((8, 128)), v((16, atoms), BF16), v((8, atoms)), v((3, atoms)),
        pltpu.SemaphoreType.DMA((atoms // head_chunk,)), pltpu.SemaphoreType.DMA((atoms // chunk,)),
        pltpu.SemaphoreType.DMA((12,)), pltpu.SemaphoreType.DMA((15,)),
        pltpu.SemaphoreType.DMA((15,)),
    ]
    sds = jax.ShapeDtypeStruct
    shapes = (
        sds((atoms, feat), BF16), sds((3, atoms), F32),
        sds((feat, hid), F32), sds((1, hid), F32),
        sds((hid, hid), F32), sds((1, hid), F32), sds((1, hid), F32),
    )
    mids = (
        shapes[0], shapes[1], sds((2, n_leaf, wrow, hid), BF16), sds((8, 128), F32),
    )
    ins = (
        positions, energy_weight.reshape(1, atoms), send_slot.reshape(1, atoms),
        tile_slot.reshape(atoms // 128, 128), box_count.reshape(1, -1), list_box.T,
        list_image.transpose(0, 2, 1), w_in, b_in.reshape(1, hid), w_mid, b_mid.reshape(1, hid),
        w_out.reshape(hid // 128, 128),
    )
    held = [
        (pltpu.SMEM if i == 4 else pltpu.VMEM)(x.shape, x.dtype) for i, x in enumerate(ins)
    ]
    mids = pl.pallas_call(
        functools.partial(kernel, n_graph, n_leaf, head_chunk, chunk, n_grp),
        out_shape=mids,
        in_specs=[any_space] * 13,
        out_specs=(any_space,) * 4,
        scratch_shapes=held + scratch,
        compiler_params=pltpu.CompilerParams(
            collective_id=0, has_side_effects=True, vmem_limit_bytes=56 * 1024 * 1024
        ),
        name="latent_charge",
    )(features, *ins)
    pieces = 4
    outs = pl.pallas_call(
        functools.partial(finish, pieces),
        out_shape=shapes,
        in_specs=[any_space] * 4,
        out_specs=(any_space,) * len(shapes),
        scratch_shapes=[v(x.shape, x.dtype) for x in mids]
        + [v(shapes[i].shape) for i in (2, 4, 3, 5, 6)]
        + [pltpu.SemaphoreType.DMA((pieces + 3,)), pltpu.SemaphoreType.DMA((pieces + 6,))],
        compiler_params=pltpu.CompilerParams(vmem_limit_bytes=56 * 1024 * 1024),
        name="results",
    )(*mids)
    fgrad, pgrad, ing, inb, midg, midb, outg = outs
    return (fgrad, pgrad, ing, inb.reshape(hid), midg, midb.reshape(hid), outg.reshape(hid))


def solution(mesh):
    placed = (
        P(("graph", "leaf"), None),
        P(None, ("graph", "leaf")),
        P(("graph", "leaf")),
        P(("graph", "leaf")),
        P(("graph", "leaf")),
        P("leaf", "graph"),
        P("leaf", None),
        P(None, "leaf", None),
        P(), P(), P(), P(), P(),
    )
    return jax.shard_map(
        body,
        mesh=mesh,
        in_specs=placed,
        out_specs=(P(("graph", "leaf"), None), P(None, ("graph", "leaf")), P(), P(), P(), P(), P()),
        check_vma=False,
    )
```
